32 devices in a mesh: groups: 2 (over x), seq: 16 (over z, y, core).
Axes of the slice: x: 2, y: 2, z: 4, core: 2. Of those that a mesh axis runs over, the one named last changes fastest.
Arguments:
- tokens: bfloat16 [4096, 768], P(('groups', 'seq')), parts along dimension 0, may hold values from -6 to 6
- gain: float32 [768], replicated, may hold values from 0.1 to 1.9
- w_qkv: bfloat16 [768, 2304], replicated, may hold values from -3 to 3
- w_out: bfloat16 [768, 768], replicated, may hold values from -0.21875 to 0.21875
- nbr_list: int32 [64, 8], P('groups'), parts along dimension 0, may hold values from 0 to 31, as said below
- nbr_count: int32 [64], P('groups'), parts along dimension 0, may hold values from 1 to 8, as said below
- cotangent: bfloat16 [4096, 768], P(('groups', 'seq')), parts along dimension 0, may hold values from -6 to 6
Outputs:
- layer_out: bfloat16 [4096, 768], P(('groups', 'seq')), parts along dimension 0
- token_grad: bfloat16 [4096, 768], P(('groups', 'seq')), parts along dimension 0
The draws below stay inside these ranges and needn't reach their ends.
There are 2 independent parts, one for each index of `groups`. The reference program is written for one: setup_inputs(seed, part) draws one part's arguments, and reference() takes and returns one part's arrays. A program takes and returns all parts, laid end to end along the dimension named above; an argument that names none is the same for every part. Nothing has to cross between parts.
Inputs may be any that keep to these rules, and one draw needn't show every extreme that they name: `nbr_list`: block c belongs to device c // 2. Entry 0 of row b is b; entries 1 to nbr_count[b] - 1 are distinct blocks, none equal to b, of devices at offsets -8 to 7 from the owner of b; the remaining entries repeat b. Over the 2 rows of one device, at most one block of each other device is named. `nbr_count`: some block has 8.
All inputs are finite; a program needn't handle non-finite values.
Results may differ from the reference program's by a relative error of at most 0.0049.
Values may be sent and summed in bfloat16 or wider, within the bound.
No kernel may reach another device: no remote copies, remote signals or barrier semaphores. Data moves between devices by JAX's collectives and lax.ppermute only.
A program may use at most 128 MiB of HBM per device.

```python
import jax
import jax.numpy as jnp
from jax import lax

HD = 64
D = 768
BLK = 64
QB = 2
MAXNB = 8
HALF = 8
NBLK = 32
TOKENS = 2048
N_SEQ = 16


def neighbour_tables(key):
    dev_count = NBLK // QB
    span = 2 * HALF
    key_pick, key_score, key_count, key_force = jax.random.split(key, 4)
    picked = jax.random.randint(key_pick, (dev_count, span), 0, QB)
    device = jnp.arange(dev_count)[:, None]
    offsets = jnp.arange(span)[None, :] - HALF
    owner = device + offsets
    usable = (owner >= 0) & (owner < dev_count) & (offsets != 0)
    peer_blocks = jnp.clip(owner, 0, dev_count - 1) * QB + picked
    own_blocks = device * QB + jnp.arange(QB)[None, :]
    candidates = jnp.concatenate([own_blocks, peer_blocks], axis=1)
    cand_ok = jnp.concatenate([jnp.ones((dev_count, QB), dtype=bool), usable], axis=1)
    width = QB + span
    raw = jax.random.randint(key_score, (dev_count, QB, width), 0, 1 << 16)
    scores = raw * 64 + jnp.arange(width)[None, None, :]
    self_col = jnp.arange(width)[None, None, :] == jnp.arange(QB)[None, :, None]
    scores = jnp.where(self_col, 1 << 30, scores)
    scores = jnp.where(cand_ok[:, None, :], scores, -1)
    best_vals, best_idx = jax.lax.top_k(scores, MAXNB)
    cand_rows = jnp.broadcast_to(candidates[:, None, :], (dev_count, QB, width))
    lists = jnp.take_along_axis(cand_rows, best_idx, axis=2).reshape(NBLK, MAXNB)
    counts = jax.random.randint(key_count, (NBLK,), 1, MAXNB + 1)
    forced = jax.random.randint(key_force, (), 0, NBLK)
    counts = jnp.where(jnp.arange(NBLK) == forced, MAXNB, counts)
    selfs = jnp.arange(NBLK)[:, None]
    lists = jnp.where(jnp.arange(MAXNB)[None, :] < counts[:, None], lists, selfs)
    return (lists.astype(jnp.int32), counts.astype(jnp.int32))


def draw_nbr_list(key, part):
    tables = neighbour_tables(key)
    return tables[0]


def draw_nbr_count(key, part):
    tables = neighbour_tables(key)
    return tables[1]


def draw_w_qkv(key, part):
    key = jax.random.fold_in(key, 5)
    key_base = jax.random.fold_in(key, 0)
    full = jnp.clip(jax.random.normal(key_base, (D, 3 * D), jnp.float32), -4.0, 4.0) * D ** (-0.5)
    full = jnp.clip(full, -3.0, 3.0)
    return full.astype(jnp.bfloat16)


def block_levels(stream_key, dims, pieces, smallest, high):
    level, own = 1.0, jax.random.fold_in(stream_key, 6)
    for axis_at, shards_of in pieces:
        steps = jnp.exp(jax.random.uniform(jax.random.fold_in(own, axis_at), (shards_of,), jnp.float32, smallest / len(pieces), high / len(pieces)))
        level = level * jnp.repeat(steps, dims[axis_at] // shards_of).reshape([-1 if axis == axis_at else 1 for axis in range(len(dims))])
    return level


def gaussian(key, extent, scale, limit, cuts=(), kind=jnp.bfloat16):
    array = scale * jax.random.normal(key, extent, jnp.float32)
    if cuts:
        array = array * block_levels(key, extent, cuts, -0.22, 0.18)
    return jnp.clip(array, -limit, limit).astype(kind)


def setup_inputs(seed: int = 0, part: int = 0) -> dict:
    key_list = jax.random.split(jax.random.key(seed), 8)
    own_keys = jax.random.split(jax.random.fold_in(key_list[7], part), 8)
    return {
        "tokens": gaussian(own_keys[0], (TOKENS, D), 1.0, 6.0, ((0, 16),)),
        "gain": jnp.clip(1.0 + 0.18 * jax.random.normal(key_list[1], (D,), jnp.float32), 0.1, 1.9),
        "w_qkv": draw_w_qkv(jax.random.fold_in(key_list[7], 71), part),
        "w_out": gaussian(key_list[3], (D, D), D ** -0.5, 0.21875),
        "nbr_list": draw_nbr_list(jax.random.fold_in(jax.random.fold_in(key_list[7], part), 71), part),
        "nbr_count": draw_nbr_count(jax.random.fold_in(jax.random.fold_in(key_list[7], part), 71), part),
        "cotangent": gaussian(own_keys[6], (TOKENS, D), 1.0, 6.0, ((0, 16),)),
    }


def normalize(tokens, gain):
    inputs = tokens.astype(jnp.float32)
    center = lax.optimization_barrier(jnp.mean(inputs, axis=-1, keepdims=True))
    spread = lax.optimization_barrier(jnp.mean((inputs - center) ** 2, axis=-1, keepdims=True))
    inv_std = lax.rsqrt(spread + 1e-05)
    unit = (inputs - center) * inv_std
    return (inputs, unit, inv_std, (unit * gain).astype(jnp.bfloat16))

def backnorm(norm_grad, unit, inv_std, gain, cotangent):
    scaled = norm_grad * gain
    centered = scaled - lax.optimization_barrier(jnp.mean(scaled, axis=-1, keepdims=True)) - unit * lax.optimization_barrier(jnp.mean(scaled * unit, axis=-1, keepdims=True))
    return (cotangent.astype(jnp.float32) + inv_std * centered).astype(jnp.bfloat16)

def attend(queries, grads, keys, counts):
    block_count, block_len, model_width = queries.shape
    slot_count = keys.shape[1]
    head_count = model_width // HD
    query_heads = queries.astype(jnp.float32).reshape(block_count, block_len, head_count, HD)
    key_heads = keys[..., :model_width].astype(jnp.float32).reshape(block_count, slot_count * block_len, head_count, HD)
    value_heads = keys[..., model_width:].astype(jnp.float32).reshape(block_count, slot_count * block_len, head_count, HD)
    live_mask = jnp.arange(slot_count)[None, :] < counts[:, None]
    live_mask = jnp.repeat(live_mask, block_len, axis=1)[:, None, None, :]
    scores = jnp.einsum('qthd,qkhd->qhtk', query_heads, key_heads) * 0.125
    scores = jnp.where(live_mask, scores, -1e+30)
    row_max = lax.optimization_barrier(jnp.max(scores, axis=-1, keepdims=True))
    weights = jnp.exp(scores - row_max)
    attn_prob = weights / lax.optimization_barrier(jnp.sum(weights, axis=-1, keepdims=True))
    prob_low = attn_prob.astype(jnp.bfloat16)
    attended = jnp.einsum('qhtk,qkhd->qthd', prob_low.astype(jnp.float32), value_heads)
    attended = attended.astype(jnp.bfloat16).reshape(block_count, block_len, model_width)
    grad_heads = grads.astype(jnp.float32).reshape(block_count, block_len, head_count, HD)
    prob_grad = jnp.einsum('qthd,qkhd->qhtk', grad_heads, value_heads)
    row_dot = lax.optimization_barrier(jnp.sum(attn_prob * prob_grad, axis=-1, keepdims=True))
    score_grad = (attn_prob * (prob_grad - row_dot) * 0.125).astype(jnp.bfloat16)
    query_grad = jnp.einsum('qhtk,qkhd->qthd', score_grad.astype(jnp.float32), key_heads)
    query_grad = query_grad.astype(jnp.bfloat16).reshape(block_count, block_len, model_width)
    key_grad = jnp.einsum('qhtk,qthd->qkhd', score_grad.astype(jnp.float32), query_heads)
    value_grad = jnp.einsum('qhtk,qthd->qkhd', prob_low.astype(jnp.float32), grad_heads)
    key_grad = key_grad.reshape(block_count, slot_count, block_len, model_width)
    value_grad = value_grad.reshape(block_count, slot_count, block_len, model_width)
    return (attended, query_grad, jnp.concatenate([key_grad, value_grad], axis=-1))

def reference(tokens, gain, w_qkv, w_out, nbr_list, nbr_count, cotangent):
    inputs, unit, inv_std, normed = normalize(tokens, gain)
    projected = jnp.dot(normed, w_qkv, preferred_element_type=jnp.float32)
    queries = projected[:, :D].astype(jnp.bfloat16)
    key_value = projected[:, D:].astype(jnp.bfloat16)
    kv_blocks = key_value.reshape(NBLK, BLK, 2 * D)
    out_grad = jnp.dot(cotangent, w_out.T, preferred_element_type=jnp.float32).astype(jnp.bfloat16)
    query_dev = queries.reshape(N_SEQ, QB, BLK, D)
    grad_dev = out_grad.reshape(N_SEQ, QB, BLK, D)
    lists_dev = nbr_list.reshape(N_SEQ, QB, MAXNB)
    counts_dev = nbr_count.reshape(N_SEQ, QB)
    window = 2 * HALF * QB
    padded = jnp.zeros((NBLK + window, BLK, 2 * D), jnp.float32)

    def step(accum, item):
        device, query_blk, grad_blk, lists_blk, counts_blk = item
        keys = kv_blocks[lists_blk]
        attended, query_grad, kv_term = attend(query_blk, grad_blk, keys, counts_blk)
        block_ids = (device - HALF) * QB + jnp.arange(window, dtype=jnp.int32)
        live_mask = jnp.arange(MAXNB)[None, :] < counts_blk[:, None]
        picker = (lists_blk[:, :, None] == block_ids[None, None, :]) & live_mask[:, :, None]
        picker = picker.astype(jnp.float32).reshape(QB * MAXNB, window)
        partial_value = jnp.einsum('mw,mbc->wbc', picker, kv_term.reshape(QB * MAXNB, BLK, 2 * D), precision=lax.Precision.HIGHEST)
        partial_value = lax.optimization_barrier(partial_value.astype(jnp.bfloat16)).astype(jnp.float32)
        start = (device * QB).astype(jnp.int32)
        current = lax.dynamic_slice_in_dim(accum, start, window, 0)
        accum = lax.dynamic_update_slice_in_dim(accum, current + partial_value, start, 0)
        return (accum, (attended, query_grad))
    devices = jnp.arange(N_SEQ, dtype=jnp.int32)
    accum, (attended, query_grad) = lax.scan(step, padded, (devices, query_dev, grad_dev, lists_dev, counts_dev))
    kv_grad = accum[HALF * QB:HALF * QB + NBLK].astype(jnp.bfloat16).reshape(TOKENS, 2 * D)
    attended = attended.reshape(TOKENS, D)
    query_grad = query_grad.reshape(TOKENS, D)
    layer_out = (inputs + jnp.dot(attended, w_out, preferred_element_type=jnp.float32)).astype(jnp.bfloat16)
    qkv_grad = jnp.concatenate([query_grad, kv_grad], axis=1)
    norm_grad = jnp.dot(qkv_grad, w_qkv.T, preferred_element_type=jnp.float32)
    token_grad = backnorm(norm_grad, unit, inv_std, gain, cotangent)
    return (layer_out, token_grad)
```

```python
import functools

import jax
import jax.numpy as jnp
from jax import lax
from jax.experimental import pallas as pl
from jax.experimental.pallas import tpu as pltpu
from jax.sharding import PartitionSpec as P

HD = 64
BLK = 64
MAXNB = 8
HALF = 8
REACH = (HALF + 1) // 2
F32 = jnp.float32
BF16 = jnp.bfloat16


def exchange_rounds(chips):
    near = lambda a, b: 0 <= b < chips and abs(a - b) <= REACH
    if chips <= 8 and chips & (chips - 1) == 0:
        masks = list(range(1, chips))
        return [
            (lambda k, m=m: k ^ m, lambda k, m=m: k ^ m, [(k, k ^ m) for k in range(chips) if near(k, k ^ m)])
            for m in masks
        ]
    shifts = [d for d in range(-REACH, REACH + 1) if d != 0]
    return [
        (lambda k, d=d: k + d, lambda k, d=d: k - d, [(k, k + d) for k in range(chips) if near(k, k + d)])
        for d in shifts
    ]


def round_of(chips, mine, peer):
    if chips <= 8 and chips & (chips - 1) == 0:
        return mine ^ peer
    d = peer - mine
    return jnp.where(d < 0, d + REACH + 1, jnp.where(d == 0, 0, d + REACH))


def layer_norm(x):
    center = jnp.mean(x, axis=-1, keepdims=True)
    spread = jnp.mean((x - center) ** 2, axis=-1, keepdims=True)
    inv_std = lax.rsqrt(spread + 1e-05)
    return (x - center) * inv_std, inv_std


def dot(a, b, ca, cb):
    return lax.dot_general(a, b, (((ca,), (cb,)), ((), ())), preferred_element_type=F32)


def main_kernel(rounds, meta, *refs):
    windows = refs[: 2 * (rounds + 1)]
    q_ref, g_ref, gain_ref, w_hbm = refs[2 * (rounds + 1) : 2 * (rounds + 1) + 4]
    outs = refs[2 * (rounds + 1) + 4 :]
    att_ref, dq_ref, own_ref, sib_ref = outs[:4]
    msg_refs = outs[4 : 4 + rounds]
    xs, normed, kv, kvt, acc, w, sems, wsem = outs[4 + rounds :]
    width = q_ref.shape[1]
    slots = 2 * MAXNB
    span = MAXNB * BLK

    wcopy = pltpu.make_async_copy(w_hbm, w, wsem)
    copies = [
        pltpu.make_async_copy(ref, xs.at[pl.ds(2 * i, 2)], sems.at[i]) for i, ref in enumerate(windows)
    ]
    for c in copies:
        c.start()
    wcopy.start()
    acc[...] = jnp.zeros_like(acc)
    for c in copies:
        c.wait()
    gain = gain_ref[...]
    for s in range(slots):
        unit, _ = layer_norm(xs[meta[s]].astype(F32))
        normed[s * BLK : (s + 1) * BLK, :] = (unit * gain).astype(BF16)
    wcopy.wait()
    rows = 256
    for i in range(slots * BLK // rows):
        part = pl.ds(i * rows, rows)
        kv[part, :] = dot(normed[part, :], w[:, width:], 1, 0).astype(BF16)

    lane = lax.broadcasted_iota(jnp.int32, (1, 2 * HD), 1)
    low = (lane < HD).astype(F32)
    high = 1.0 - low
    slot_row = lax.broadcasted_iota(jnp.int32, (span, 1), 0)
    for b in range(2):
        live = slot_row < meta[2 * slots + b] * BLK
        for p in range(width // (2 * HD)):
            lanes = pl.ds(p * 2 * HD, 2 * HD)
            vlanes = pl.ds(width + p * 2 * HD, 2 * HD)
            tok = pl.ds(b * BLK, BLK)
            krows = pl.ds(b * span, span)
            q = q_ref[tok, lanes].astype(F32) * 0.125
            g = g_ref[tok, lanes].astype(F32)
            qd = jnp.concatenate([q * low, q * high], axis=0).astype(BF16)
            gd = jnp.concatenate([g * low, g * high], axis=0).astype(BF16)
            k = kv[krows, lanes]
            v = kv[krows, vlanes]
            scores = jnp.where(live, dot(k, qd, 1, 1), -1e30)
            weights = jnp.exp(scores - jnp.max(scores, axis=0, keepdims=True))
            prob = weights * (1.0 / jnp.sum(weights, axis=0, keepdims=True))
            low_prob = prob.astype(BF16)
            pg = dot(v, gd, 1, 1)
            row_dot = jnp.sum(prob * pg, axis=0, keepdims=True)
            sg = (prob * (pg - row_dot)).astype(BF16)
            kvt[krows, lanes] = dot(sg, qd, 1, 0).astype(BF16)
            kvt[krows, vlanes] = dot(low_prob, gd, 1, 0).astype(BF16)
            att = dot(low_prob, v, 0, 0)
            dq = dot(sg, k, 0, 0) * 0.125
            att_ref[tok, lanes] = jnp.where(lane < HD, att[:BLK], att[BLK:]).astype(BF16)
            dq_ref[tok, lanes] = jnp.where(lane < HD, dq[:BLK], dq[BLK:]).astype(BF16)

    for i in range(slots * BLK // rows):
        part = dot(kvt[pl.ds(i * rows, rows), :], w[:, width:], 1, 1)
        for j in range(rows // BLK):
            at = meta[slots + i * (rows // BLK) + j]
            acc[at] = acc[at] + part[j * BLK : (j + 1) * BLK, :]
    own_ref[0:BLK, :] = acc[0]
    own_ref[BLK : 2 * BLK, :] = acc[1]
    sib_ref[...] = acc[2].astype(BF16)
    for r in range(rounds):
        msg_refs[r][0:BLK, :] = acc[3 + 2 * r].astype(BF16)
        msg_refs[r][BLK : 2 * BLK, :] = acc[4 + 2 * r].astype(BF16)


def main_call(meta, windows, queries, grads, gain, w_qkv):
    rounds = len(windows) // 2 - 1
    tokens, width = queries.shape
    any_spec = pl.BlockSpec(memory_space=pl.ANY)
    vmem = pl.BlockSpec(memory_space=pltpu.VMEM)
    slots = 2 * MAXNB
    outs = [
        jax.ShapeDtypeStruct((tokens, width), BF16),
        jax.ShapeDtypeStruct((tokens, width), BF16),
        jax.ShapeDtypeStruct((tokens, width), F32),
        jax.ShapeDtypeStruct((BLK, width), BF16),
    ] + [jax.ShapeDtypeStruct((2 * BLK, width), BF16)] * rounds
    return pl.pallas_call(
        functools.partial(main_kernel, rounds),
        out_shape=outs,
        in_specs=[pl.BlockSpec(memory_space=pltpu.SMEM)] + [any_spec] * len(windows) + [vmem] * 3 + [any_spec],
        out_specs=[vmem] * len(outs),
        scratch_shapes=[
            pltpu.VMEM((2 * len(windows), BLK, width), BF16),
            pltpu.VMEM((slots * BLK, width), BF16),
            pltpu.VMEM((slots * BLK, 2 * width), BF16),
            pltpu.VMEM((slots * BLK, 2 * width), BF16),
            pltpu.VMEM((4 + 2 * rounds, BLK, width), F32),
            pltpu.VMEM(w_qkv.shape, BF16),
            pltpu.SemaphoreType.DMA((len(windows),)),
            pltpu.SemaphoreType.DMA,
        ],
        compiler_params=pltpu.CompilerParams(vmem_limit_bytes=48 * 2**20),
        cost_estimate=pl.CostEstimate(flops=8 * 10**9, bytes_accessed=12 * 10**6, transcendentals=10**6),
    )(meta, *[x.reshape(2, BLK, width) for x in windows], queries, grads, gain.reshape(1, width), w_qkv)


def final_kernel(rounds, parity, *refs):
    came = refs[:rounds]
    sibs, sib, base, tok_ref, cot_ref, gain_ref, out_ref, total = refs[rounds:]
    total[...] = base[...]
    one = sib[...].astype(F32)
    total[parity[0]] = total[parity[0]] + one
    for r in range(rounds):
        at = parity[1 + r]
        total[at] = total[at] + came[r][0:BLK, :].astype(F32)
        at = parity[1 + rounds + r]
        total[at] = total[at] + sibs[r * BLK : (r + 1) * BLK, :].astype(F32)
    gain = gain_ref[...]
    for b in range(2):
        rows = pl.ds(b * BLK, BLK)
        unit, inv_std = layer_norm(tok_ref[rows, :].astype(F32))
        scaled = total[b] * gain
        centered = (
            scaled
            - jnp.mean(scaled, axis=-1, keepdims=True)
            - unit * jnp.mean(scaled * unit, axis=-1, keepdims=True)
        )
        out_ref[rows, :] = (cot_ref[rows, :].astype(F32) + inv_std * centered).astype(BF16)


def final_call(parity, came, sibs, sib, base, tokens, cotangent, gain):
    rounds = len(came)
    count, width = tokens.shape
    vmem = pl.BlockSpec(memory_space=pltpu.VMEM)
    return pl.pallas_call(
        functools.partial(final_kernel, rounds),
        out_shape=jax.ShapeDtypeStruct((count, width), BF16),
        in_specs=[pl.BlockSpec(memory_space=pltpu.SMEM)] + [vmem] * (rounds + 6),
        out_specs=vmem,
        scratch_shapes=[pltpu.VMEM((2, BLK, width), F32)],
        compiler_params=pltpu.CompilerParams(vmem_limit_bytes=32 * 2**20),
    )(parity, *came, sibs, sib, base.reshape(2, BLK, width), tokens, cotangent, gain.reshape(1, width))


def per_device(tokens, gain, w_qkv, w_out, nbr_list, nbr_count, cotangent):
    devices = lax.axis_size("seq")
    chips = devices // 2
    count, width = tokens.shape
    blocks = count // BLK
    plan = exchange_rounds(chips)
    rounds = len(plan)
    mate = [(i, i ^ 1) for i in range(devices)]

    def fetch(x, pairs):
        return lax.ppermute(x, "seq", [(2 * s + c, 2 * r + c) for r, s in pairs for c in range(2)])

    def give(x, pairs):
        return lax.ppermute(x, "seq", [(2 * r + c, 2 * s + c) for r, s in pairs for c in range(2)])

    arrived = [None] * rounds
    for r in reversed(range(rounds)):
        arrived[r] = fetch(tokens, plan[r][2])
    windows = [tokens, lax.ppermute(tokens, "seq", mate)]
    for r in range(rounds):
        windows += [arrived[r], lax.ppermute(arrived[r], "seq", mate)]

    position = lax.axis_index("seq")
    chip, core = position // 2, position % 2
    my_lists = lax.dynamic_slice_in_dim(nbr_list, position * blocks, blocks, 0)
    my_counts = lax.dynamic_slice_in_dim(nbr_count, position * blocks, blocks, 0)
    owner = my_lists // blocks
    block = my_lists % blocks
    turn = round_of(chips, chip, owner // 2)
    other = (owner % 2) ^ core
    source = (turn * 2 + other) * 2 + block
    target = jnp.where(owner == position, block, 1 + 2 * turn + other)
    live = jnp.arange(MAXNB)[None, :] < my_counts[:, None]
    target = jnp.where(live, target, 3 + 2 * rounds)
    meta = jnp.concatenate([source.reshape(-1), target.reshape(-1), my_counts]).astype(jnp.int32)

    all_live = jnp.arange(MAXNB)[None, :] < nbr_count[:, None]
    names_odd = jnp.any((all_live & (nbr_list == position * blocks + 1)).reshape(devices, -1), axis=1)
    givers = jnp.stack([position ^ 1] + [plan[r][1](chip) * 2 + core for r in range(rounds)]
                       + [plan[r][1](chip) * 2 + (1 - core) for r in range(rounds)])
    parity = jnp.take(names_odd.astype(jnp.int32), jnp.clip(givers, 0, devices - 1))

    unit, _ = layer_norm(tokens.astype(F32))
    normed = (unit * gain).astype(BF16)
    queries = jnp.dot(normed, w_qkv[:, :width], preferred_element_type=F32).astype(BF16)
    out_grad = dot(cotangent, w_out, 1, 1).astype(BF16)

    attended, query_grad, own, sib, *messages = main_call(meta, windows, queries, out_grad, gain, w_qkv)

    sib = lax.ppermute(sib, "seq", mate)
    came = [None] * rounds
    for r in reversed(range(rounds)):
        came[r] = give(messages[r], plan[r][2])
    sibs = lax.ppermute(jnp.concatenate([x[BLK:] for x in came], axis=0), "seq", mate)
    layer_out = (tokens.astype(F32) + jnp.dot(attended, w_out, preferred_element_type=F32)).astype(BF16)
    base = own + dot(query_grad, w_qkv[:, :width], 1, 1)
    token_grad = final_call(parity, came, sibs, sib, base, tokens, cotangent, gain)
    return (layer_out, token_grad)


def solution(mesh):
    in_specs = (
        P(("groups", "seq"), None),
        P(),
        P(),
        P(),
        P("groups", None),
        P("groups"),
        P(("groups", "seq"), None),
    )
    out_specs = (P(("groups", "seq"), None), P(("groups", "seq"), None))
    return jax.shard_map(
        per_device, mesh=mesh, in_specs=in_specs, out_specs=out_specs, check_vma=False
    )
```

```python
import functools

import jax
import jax.numpy as jnp
from jax import lax
from jax.experimental import pallas as pl
from jax.experimental.pallas import tpu as pltpu
from jax.sharding import PartitionSpec as P

HD = 64
BLK = 64
MAXNB = 8
HALF = 8
REACH = (HALF + 1) // 2
F32 = jnp.float32
BF16 = jnp.bfloat16


class Round:
    def __init__(self, fetch, source, give, giver):
        self.fetch, self.source, self.give, self.giver = fetch, source, give, giver


def exchange_rounds(chips):
    near = lambda a, b: 0 <= a < chips and 0 <= b < chips and abs(a - b) <= REACH
    if chips == 8:
        rounds = []
        for m in range(1, 8):
            pairs = [(k, k ^ m) for k in range(chips) if near(k, k ^ m)]
            relay = m in (3, 5, 7)
            fetch = [(k, k ^ 1) for k, _ in pairs] if relay else pairs
            rounds.append(Round(fetch, (m ^ 1) - 1 if relay else None, pairs, lambda k, m=m: k ^ m))
        return rounds, [5, 1, 3, 0, 2, 6, 4], [3, 5, 4, 6, 2, 1, 0]
    rounds = []
    for d in range(-REACH, REACH + 1):
        if d != 0:
            pairs = [(k, k + d) for k in range(chips) if near(k, k + d)]
            rounds.append(Round(pairs, None, [(s, r) for r, s in pairs], lambda k, d=d: k - d))
    return rounds, list(range(len(rounds))), list(range(len(rounds)))


def round_of(chips, mine, peer):
    if chips == 8:
        return mine ^ peer
    d = peer - mine
    return jnp.where(d < 0, d + REACH + 1, jnp.where(d == 0, 0, d + REACH))


def layer_norm(x):
    center = jnp.mean(x, axis=-1, keepdims=True)
    spread = jnp.mean((x - center) ** 2, axis=-1, keepdims=True)
    inv_std = lax.rsqrt(spread + 1e-05)
    return (x - center) * inv_std, inv_std


def dot(a, b, ca, cb):
    return lax.dot_general(a, b, (((ca,), (cb,)), ((), ())), preferred_element_type=F32)


def call(kernel, out_shape, in_specs, out_specs, scratch, mib, flops=0):
    return pl.pallas_call(
        kernel,
        out_shape=out_shape,
        in_specs=in_specs,
        out_specs=out_specs,
        scratch_shapes=scratch,
        compiler_params=pltpu.CompilerParams(vmem_limit_bytes=mib * 2**20),
        cost_estimate=pl.CostEstimate(flops=flops, bytes_accessed=5 * 10**6, transcendentals=0),
    )


SMEM = pl.BlockSpec(memory_space=pltpu.SMEM)
VMEM = pl.BlockSpec(memory_space=pltpu.VMEM)
ANY = pl.BlockSpec(memory_space=pl.ANY)
HBM = pl.BlockSpec(memory_space=pltpu.HBM)


def weight_copies(source, target, sems):
    rows, columns = target.shape
    band = rows // sems.shape[0]
    from_column = source.shape[1] - columns
    return [
        pltpu.make_async_copy(
            source.at[pl.ds(i * band, band), pl.ds(from_column, columns)],
            target.at[pl.ds(i * band, band)],
            sems.at[i],
        )
        for i in range(sems.shape[0])
    ]


def main_kernel(rounds, meta, *refs):
    count = 2 * (rounds + 1)
    windows = refs[:count]
    q_ref, g_ref, gain_ref, w_hbm = refs[count : count + 4]
    att_ref, dq_ref, own_ref, sib_ref = refs[count + 4 : count + 8]
    msg_refs = refs[count + 8 : count + 8 + rounds]
    normed, kv, kvt, acc, stage, w, msems, wsems = refs[count + 8 + rounds :]
    width = q_ref.shape[1]
    wcopies = weight_copies(w_hbm, w, wsems)
    for c in wcopies:
        c.start()
    slots = 2 * MAXNB
    span = MAXNB * BLK

    gain = gain_ref[...]
    for i in range(count):
        for j in range(2):

            @pl.when(meta[2 * slots + 2 + 2 * i + j] != 0)
            def _():
                unit, _ = layer_norm(windows[i][j * BLK : (j + 1) * BLK, :].astype(F32))
                normed[2 * i + j] = (unit * gain).astype(BF16)

    for c in wcopies:
        c.wait()
    rows = 256
    for i in range(slots * BLK // rows):
        part = jnp.concatenate([normed[meta[4 * i + j]] for j in range(4)], axis=0)
        kv[pl.ds(i * rows, rows), :] = dot(part, w[...], 1, 0).astype(BF16)
    acc[...] = jnp.zeros_like(acc)

    lane = lax.broadcasted_iota(jnp.int32, (1, 2 * HD), 1)
    low = (lane < HD).astype(F32)
    high = 1.0 - low
    slot_row = lax.broadcasted_iota(jnp.int32, (span, 1), 0)
    for b in range(2):
        live = slot_row < meta[2 * slots + b] * BLK
        for p in range(width // (2 * HD)):
            lanes = pl.ds(p * 2 * HD, 2 * HD)
            vlanes = pl.ds(width + p * 2 * HD, 2 * HD)
            tok = pl.ds(b * BLK, BLK)
            krows = pl.ds(b * span, span)
            q = q_ref[tok, lanes].astype(F32) * 0.125
            g = g_ref[tok, lanes].astype(F32)
            qd = jnp.concatenate([q * low, q * high], axis=0).astype(BF16)
            gd = jnp.concatenate([g * low, g * high], axis=0).astype(BF16)
            k = kv[krows, lanes]
            v = kv[krows, vlanes]
            scores = jnp.where(live, dot(k, qd, 1, 1), -1e30)
            weights = jnp.exp(scores - jnp.max(scores, axis=0, keepdims=True))
            prob = weights * (1.0 / jnp.sum(weights, axis=0, keepdims=True))
            low_prob = prob.astype(BF16)
            pg = dot(v, gd, 1, 1)
            row_dot = jnp.sum(prob * pg, axis=0, keepdims=True)
            sg = (prob * (pg - row_dot)).astype(BF16)
            kvt[krows, lanes] = dot(sg, qd, 1, 0).astype(BF16)
            kvt[krows, vlanes] = dot(low_prob, gd, 1, 0).astype(BF16)
            att = dot(low_prob, v, 0, 0)
            dq = dot(sg, k, 0, 0) * 0.125
            att_ref[tok, lanes] = jnp.where(lane < HD, att[:BLK], att[BLK:]).astype(BF16)
            dq_ref[tok, lanes] = jnp.where(lane < HD, dq[:BLK], dq[BLK:]).astype(BF16)

    for i in range(slots * BLK // rows):
        part = dot(kvt[pl.ds(i * rows, rows), :], w[...], 1, 1)
        for j in range(rows // BLK):
            at = meta[slots + i * (rows // BLK) + j]
            acc[at] = acc[at] + part[j * BLK : (j + 1) * BLK, :]
    for r in range(rounds):
        stage[r, 0:BLK, :] = acc[3 + 2 * r].astype(BF16)
        stage[r, BLK : 2 * BLK, :] = acc[4 + 2 * r].astype(BF16)
        pltpu.make_async_copy(stage.at[r], msg_refs[r], msems.at[r]).start()
    own_ref[0:BLK, :] = acc[0]
    own_ref[BLK : 2 * BLK, :] = acc[1]
    sib_ref[...] = acc[2].astype(BF16)
    for r in range(rounds):
        pltpu.make_async_copy(stage.at[r], msg_refs[r], msems.at[r]).wait()


def main_call(meta, windows, queries, grads, gain, w_qkv):
    rounds = len(windows) // 2 - 1
    tokens, width = queries.shape
    slots = 2 * MAXNB
    shape = jax.ShapeDtypeStruct
    return call(
        functools.partial(main_kernel, rounds),
        [shape((tokens, width), BF16)] * 2
        + [shape((tokens, width), F32), shape((BLK, width), BF16)]
        + [shape((2 * BLK, width), BF16)] * rounds,
        [SMEM] + [VMEM] * (len(windows) + 3) + [ANY],
        [VMEM] * 4 + [HBM] * rounds,
        [
            pltpu.VMEM((2 * len(windows), BLK, width), BF16),
            pltpu.VMEM((slots * BLK, 2 * width), BF16),
            pltpu.VMEM((slots * BLK, 2 * width), BF16),
            pltpu.VMEM((4 + 2 * rounds, BLK, width), F32),
            pltpu.VMEM((rounds, 2 * BLK, width), BF16),
            pltpu.VMEM((width, 2 * width), BF16),
            pltpu.SemaphoreType.DMA((rounds,)),
            pltpu.SemaphoreType.DMA((6,)),
        ],
        48,
        8 * 10**9,
    )(meta, *windows, queries, grads, gain, w_qkv)


def add_came(total, came, at, rows):
    total[at] = total[at] + came[rows, :].astype(F32)


def middle_kernel(rows_of, parity, came, *refs):
    att_ref, dq_ref, own_ref, tok_ref, wqkv_hbm, wout_hbm, out_ref, total, wq, wout, sems = refs
    width = tok_ref.shape[1]
    copies = [
        pltpu.make_async_copy(wout_hbm, wout, sems.at[0]),
        pltpu.make_async_copy(wqkv_hbm.at[:, pl.ds(0, width)], wq, sems.at[1]),
    ]
    for c in copies:
        c.start()
    for c in copies:
        c.wait()
    out = tok_ref[...].astype(F32) + dot(att_ref[...], wout[...], 1, 0)
    out_ref[...] = out.astype(BF16)
    base = own_ref[...] + dot(dq_ref[...], wq[...], 1, 1)
    for b in range(2):
        total[b] = base[b * BLK : (b + 1) * BLK, :]
    add_came(total, came, parity[rows_of], pl.ds(0, BLK))


def middle_call(rows_of, parity, came, attended, query_grad, own, tokens, w_qkv, w_out):
    count, width = tokens.shape
    return call(
        functools.partial(middle_kernel, rows_of),
        [jax.ShapeDtypeStruct((count, width), BF16), jax.ShapeDtypeStruct((2, BLK, width), F32)],
        [SMEM] + [VMEM] * 5 + [ANY] * 2,
        [VMEM] * 2,
        [pltpu.VMEM((width, width), BF16)] * 2 + [pltpu.SemaphoreType.DMA((2,))],
        48,
    )(parity, came, attended, query_grad, own, tokens, w_qkv, w_out)


def final_kernel(rounds, done, parity, *refs):
    came, sibs = refs[:rounds], refs[rounds : 2 * rounds]
    sib, base, tok_ref, cot_ref, gain_ref, out_ref, total = refs[2 * rounds :]
    total[...] = base[...]
    add_came(total, sib, parity[0], pl.ds(0, BLK))
    for r in range(rounds):
        if r != done:
            add_came(total, came[r], parity[1 + r], pl.ds(0, BLK))
        add_came(total, sibs[r], parity[1 + rounds + r], pl.ds(BLK, BLK))
    gain = gain_ref[...]
    for b in range(2):
        rows = pl.ds(b * BLK, BLK)
        unit, inv_std = layer_norm(tok_ref[rows, :].astype(F32))
        scaled = total[b] * gain
        centered = (
            scaled
            - jnp.mean(scaled, axis=-1, keepdims=True)
            - unit * jnp.mean(scaled * unit, axis=-1, keepdims=True)
        )
        out_ref[rows, :] = (cot_ref[rows, :].astype(F32) + inv_std * centered).astype(BF16)


def final_call(done, parity, came, sibs, sib, base, tokens, cotangent, gain):
    rounds = len(came)
    count, width = tokens.shape
    return call(
        functools.partial(final_kernel, rounds, done),
        jax.ShapeDtypeStruct((count, width), BF16),
        [SMEM] + [VMEM] * (2 * rounds + 5),
        VMEM,
        [pltpu.VMEM((2, BLK, width), F32)],
        8,
    )(parity, *came, *sibs, sib, base, tokens, cotangent, gain)


def per_device(tokens, gain, w_qkv, w_out, nbr_list, nbr_count, cotangent):
    devices = lax.axis_size("seq")
    chips = devices // 2
    count, width = tokens.shape
    blocks = count // BLK
    plan, fetch_order, give_order = exchange_rounds(chips)
    rounds = len(plan)
    mate = [(i, i ^ 1) for i in range(devices)]

    def send(x, pairs):
        return lax.ppermute(x, "seq", [(2 * s + c, 2 * r + c) for r, s in pairs for c in range(2)])

    arrived, passed = [None] * rounds, [None] * rounds
    for r in fetch_order:
        source = plan[r].source
        arrived[r] = send(tokens if source is None else arrived[source], plan[r].fetch)
    for r in fetch_order:
        passed[r] = lax.ppermute(arrived[r], "seq", mate)
    windows = [tokens, lax.ppermute(tokens, "seq", mate)]
    for r in range(rounds):
        windows += [arrived[r], passed[r]]

    position = lax.axis_index("seq")
    chip, core = position // 2, position % 2
    my_lists = lax.dynamic_slice_in_dim(nbr_list, position * blocks, blocks, 0)
    my_counts = lax.dynamic_slice_in_dim(nbr_count, position * blocks, blocks, 0)
    owner = my_lists // blocks
    block = my_lists % blocks
    turn = round_of(chips, chip, owner // 2)
    other = (owner % 2) ^ core
    source = (turn * 2 + other) * 2 + block
    target = jnp.where(owner == position, block, 1 + 2 * turn + other)
    live = jnp.arange(MAXNB)[None, :] < my_counts[:, None]
    target = jnp.where(live, target, 3 + 2 * rounds)
    named = jnp.any(source.reshape(-1, 1) == jnp.arange(4 * (rounds + 1))[None, :], axis=0)
    meta = jnp.concatenate([source.reshape(-1), target.reshape(-1), my_counts, named]).astype(jnp.int32)

    all_live = jnp.arange(MAXNB)[None, :] < nbr_count[:, None]
    names_odd = jnp.any((all_live & (nbr_list == position * blocks + 1)).reshape(devices, -1), axis=1)
    givers = jnp.stack([position ^ 1] + [plan[r].giver(chip) * 2 + core for r in range(rounds)]
                       + [plan[r].giver(chip) * 2 + (1 - core) for r in range(rounds)])
    parity = jnp.take(names_odd.astype(jnp.int32), jnp.clip(givers, 0, devices - 1))

    gain = gain.reshape(1, width)
    unit, _ = layer_norm(tokens.astype(F32))
    normed = (unit * gain).astype(BF16)
    queries = jnp.dot(normed, w_qkv[:, :width], preferred_element_type=F32).astype(BF16)
    out_grad = dot(cotangent, w_out, 1, 1).astype(BF16)
    attended, query_grad, own, sib, *messages = main_call(meta, windows, queries, out_grad, gain, w_qkv)

    sib = lax.ppermute(sib, "seq", mate)
    came, sibs = [None] * rounds, [None] * rounds
    first, last = give_order[0], give_order[-1]
    for r in give_order:
        if r == last:
            layer_out, base = middle_call(
                1 + first, parity, came[first], attended, query_grad, own, tokens, w_qkv, w_out
            )
            messages[r], layer_out, base = lax.optimization_barrier((messages[r], layer_out, base))
        came[r] = send(messages[r], plan[r].give)
    for r in give_order:
        sibs[r] = lax.ppermute(came[r], "seq", mate)
    token_grad = final_call(first, parity, came, sibs, sib, base, tokens, cotangent, gain)
    return (layer_out, token_grad)


def solution(mesh):
    in_specs = (
        P(("groups", "seq"), None),
        P(),
        P(),
        P(),
        P("groups", None),
        P("groups"),
        P(("groups", "seq"), None),
    )
    out_specs = (P(("groups", "seq"), None), P(("groups", "seq"), None))
    return jax.shard_map(
        per_device, mesh=mesh, in_specs=in_specs, out_specs=out_specs, check_vma=False
    )
```

```python
import functools

import jax
import jax.numpy as jnp
from jax import lax
from jax.experimental import pallas as pl
from jax.experimental.pallas import tpu as pltpu
from jax.sharding import PartitionSpec as P

HD = 64
BLK = 64
MAXNB = 8
HALF = 8
PACK = 4
REACH = (HALF + 1) // 2
F32 = jnp.float32
BF16 = jnp.bfloat16


class Round:
    def __init__(self, fetch, source, give, giver):
        self.fetch, self.source, self.give, self.giver = fetch, source, give, giver


def exchange_rounds(chips):
    near = lambda a, b: 0 <= a < chips and 0 <= b < chips and abs(a - b) <= REACH
    if chips == 8:
        rounds = []
        for m in range(1, 8):
            pairs = [(k, k ^ m) for k in range(chips) if near(k, k ^ m)]
            relay = m in (3, 5, 7)
            fetch = [(k, k ^ 1) for k, _ in pairs] if relay else pairs
            rounds.append(Round(fetch, (m ^ 1) - 1 if relay else None, pairs, lambda k, m=m: k ^ m))
        return rounds, [5, 0, 3, 1, 2, 6, 4], [3, 1, 0, 4, 2, 5, 6]
    rounds = []
    for d in range(-REACH, REACH + 1):
        if d != 0:
            pairs = [(k, k + d) for k in range(chips) if near(k, k + d)]
            rounds.append(Round(pairs, None, [(s, r) for r, s in pairs], lambda k, d=d: k - d))
    return rounds, list(range(len(rounds))), list(range(len(rounds)))


def round_of(chips, mine, peer):
    if chips == 8:
        return mine ^ peer
    d = peer - mine
    return jnp.where(d < 0, d + REACH + 1, jnp.where(d == 0, 0, d + REACH))


def layer_norm(x):
    center = jnp.mean(x, axis=-1, keepdims=True)
    spread = jnp.mean((x - center) ** 2, axis=-1, keepdims=True)
    inv_std = lax.rsqrt(spread + 1e-05)
    return (x - center) * inv_std, inv_std


def dot(a, b, ca, cb):
    return lax.dot_general(a, b, (((ca,), (cb,)), ((), ())), preferred_element_type=F32)


def call(kernel, out_shape, in_specs, out_specs, scratch, mib, flops=0):
    return pl.pallas_call(
        kernel,
        out_shape=out_shape,
        in_specs=in_specs,
        out_specs=out_specs,
        scratch_shapes=scratch,
        compiler_params=pltpu.CompilerParams(vmem_limit_bytes=mib * 2**20),
        cost_estimate=pl.CostEstimate(flops=flops, bytes_accessed=5 * 10**6, transcendentals=0),
    )


SMEM = pl.BlockSpec(memory_space=pltpu.SMEM)
VMEM = pl.BlockSpec(memory_space=pltpu.VMEM)
ANY = pl.BlockSpec(memory_space=pl.ANY)


def weight_copies(source, target, sems):
    rows, columns = target.shape
    band = rows // sems.shape[0]
    from_column = source.shape[1] - columns
    return [
        pltpu.make_async_copy(
            source.at[pl.ds(i * band, band), pl.ds(from_column, columns)],
            target.at[pl.ds(i * band, band)],
            sems.at[i],
        )
        for i in range(sems.shape[0])
    ]


def main_kernel(rounds, places, meta, *refs):
    count = len(places)
    windows = refs[:count]
    q_ref, g_ref, gain_ref, w_hbm = refs[count : count + 4]
    att_ref, dq_ref, own_ref, sib_ref = refs[count + 4 : count + 8]
    msg_refs = refs[count + 8 : count + 8 + rounds]
    normed, kv, kvt, acc, w, wsems = refs[count + 8 + rounds :]
    width = q_ref.shape[1]
    wcopies = weight_copies(w_hbm, w, wsems)
    for c in wcopies:
        c.start()
    slots = 2 * MAXNB
    span = MAXNB * BLK

    gain = gain_ref[...]
    for ref, place in zip(windows, places):
        for j in range(2):

            @pl.when(meta[2 * slots + 2 + 2 * place + j] != 0)
            def _():
                unit, _ = layer_norm(ref[j * BLK : (j + 1) * BLK, :].astype(F32))
                normed[2 * place + j] = (unit * gain).astype(BF16)

    for c in wcopies:
        c.wait()
    rows = 256
    for i in range(slots * BLK // rows):
        part = jnp.concatenate([normed[meta[4 * i + j]] for j in range(4)], axis=0)
        kv[pl.ds(i * rows, rows), :] = dot(part, w[...], 1, 0).astype(BF16)
    acc[...] = jnp.zeros_like(acc)

    group = PACK * HD
    lane = lax.broadcasted_iota(jnp.int32, (1, group), 1)
    masks = [(lane // HD == h).astype(BF16) for h in range(PACK)]
    slot_row = lax.broadcasted_iota(jnp.int32, (span, 1), 0)

    def diagonal(x):
        out = x[:BLK]
        for h in range(1, PACK):
            out = jnp.where(lane < h * HD, out, x[h * BLK : (h + 1) * BLK])
        return out

    for b in range(2):
        live = slot_row < meta[2 * slots + b] * BLK
        for p in range(width // group):
            lanes = pl.ds(p * group, group)
            vlanes = pl.ds(width + p * group, group)
            tok = pl.ds(b * BLK, BLK)
            krows = pl.ds(b * span, span)
            q = q_ref[tok, lanes] * 0.125
            g = g_ref[tok, lanes]
            qd = jnp.concatenate([q * m for m in masks], axis=0)
            gd = jnp.concatenate([g * m for m in masks], axis=0)
            k = kv[krows, lanes]
            v = kv[krows, vlanes]
            scores = jnp.where(live, dot(k, qd, 1, 1), -1e30)
            weights = jnp.exp(scores - jnp.max(scores, axis=0, keepdims=True))
            prob = weights * (1.0 / jnp.sum(weights, axis=0, keepdims=True))
            low_prob = prob.astype(BF16)
            pg = dot(v, gd, 1, 1)
            row_dot = jnp.sum(prob * pg, axis=0, keepdims=True)
            sg = (prob * (pg - row_dot)).astype(BF16)
            kvt[krows, lanes] = dot(sg, qd, 1, 0).astype(BF16)
            kvt[krows, vlanes] = dot(low_prob, gd, 1, 0).astype(BF16)
            att_ref[tok, lanes] = diagonal(dot(low_prob, v, 0, 0)).astype(BF16)
            dq_ref[tok, lanes] = (diagonal(dot(sg, k, 0, 0)) * 0.125).astype(BF16)

    for i in range(slots * BLK // rows):
        part = dot(kvt[pl.ds(i * rows, rows), :], w[...], 1, 1)
        for j in range(rows // BLK):
            at = meta[slots + i * (rows // BLK) + j]
            acc[at] = acc[at] + part[j * BLK : (j + 1) * BLK, :]
    for r in range(rounds):
        msg_refs[r][0:BLK, :] = acc[3 + 2 * r].astype(BF16)
        msg_refs[r][BLK : 2 * BLK, :] = acc[4 + 2 * r].astype(BF16)
    own_ref[0:BLK, :] = acc[0]
    own_ref[BLK : 2 * BLK, :] = acc[1]
    sib_ref[...] = acc[2].astype(BF16)


def main_call(meta, places, windows, queries, grads, gain, w_qkv):
    rounds = len(windows) // 2 - 1
    tokens, width = queries.shape
    slots = 2 * MAXNB
    shape = jax.ShapeDtypeStruct
    return call(
        functools.partial(main_kernel, rounds, places),
        [shape((tokens, width), BF16)] * 2
        + [shape((tokens, width), F32), shape((BLK, width), BF16)]
        + [shape((2 * BLK, width), BF16)] * rounds,
        [SMEM] + [VMEM] * (len(windows) + 3) + [ANY],
        [VMEM] * (4 + rounds),
        [
            pltpu.VMEM((2 * len(windows), BLK, width), BF16),
            pltpu.VMEM((slots * BLK, 2 * width), BF16),
            pltpu.VMEM((slots * BLK, 2 * width), BF16),
            pltpu.VMEM((4 + 2 * rounds, BLK, width), F32),
            pltpu.VMEM((width, 2 * width), BF16),
            pltpu.SemaphoreType.DMA((6,)),
        ],
        48,
        8 * 10**9,
    )(meta, *windows, queries, grads, gain, w_qkv)


def add_came(total, came, at, rows):
    total[at] = total[at] + came[rows, :].astype(F32)


def middle_kernel(rows_of, parity, came, *refs):
    att_ref, dq_ref, own_ref, tok_ref, wqkv_hbm, wout_hbm, out_ref, total, wq, wout, sems = refs
    width = tok_ref.shape[1]
    copies = [
        pltpu.make_async_copy(wout_hbm, wout, sems.at[0]),
        pltpu.make_async_copy(wqkv_hbm.at[:, pl.ds(0, width)], wq, sems.at[1]),
    ]
    for c in copies:
        c.start()
    for c in copies:
        c.wait()
    out = tok_ref[...].astype(F32) + dot(att_ref[...], wout[...], 1, 0)
    out_ref[...] = out.astype(BF16)
    base = own_ref[...] + dot(dq_ref[...], wq[...], 1, 1)
    for b in range(2):
        total[b] = base[b * BLK : (b + 1) * BLK, :]
    add_came(total, came, parity[rows_of], pl.ds(0, BLK))


def middle_call(rows_of, parity, came, attended, query_grad, own, tokens, w_qkv, w_out):
    count, width = tokens.shape
    return call(
        functools.partial(middle_kernel, rows_of),
        [jax.ShapeDtypeStruct((count, width), BF16), jax.ShapeDtypeStruct((2, BLK, width), F32)],
        [SMEM] + [VMEM] * 5 + [ANY] * 2,
        [VMEM] * 2,
        [pltpu.VMEM((width, width), BF16)] * 2 + [pltpu.SemaphoreType.DMA((2,))],
        48,
    )(parity, came, attended, query_grad, own, tokens, w_qkv, w_out)


def final_kernel(order, done, parity, *refs):
    rounds = len(order)
    came, sibs = dict(zip(order, refs[:rounds])), dict(zip(order, refs[rounds : 2 * rounds]))
    sib, base, tok_ref, cot_ref, gain_ref, out_ref, total = refs[2 * rounds :]
    total[...] = base[...]
    add_came(total, sib, parity[0], pl.ds(0, BLK))
    for r in range(rounds):
        if r != done:
            add_came(total, came[r], parity[1 + r], pl.ds(0, BLK))
        add_came(total, sibs[r], parity[1 + rounds + r], pl.ds(BLK, BLK))
    gain = gain_ref[...]
    for b in range(2):
        rows = pl.ds(b * BLK, BLK)
        unit, inv_std = layer_norm(tok_ref[rows, :].astype(F32))
        scaled = total[b] * gain
        centered = (
            scaled
            - jnp.mean(scaled, axis=-1, keepdims=True)
            - unit * jnp.mean(scaled * unit, axis=-1, keepdims=True)
        )
        out_ref[rows, :] = (cot_ref[rows, :].astype(F32) + inv_std * centered).astype(BF16)


def final_call(order, done, parity, came, sibs, sib, base, tokens, cotangent, gain):
    rounds = len(came)
    count, width = tokens.shape
    return call(
        functools.partial(final_kernel, order, done),
        jax.ShapeDtypeStruct((count, width), BF16),
        [SMEM] + [VMEM] * (2 * rounds + 5),
        VMEM,
        [pltpu.VMEM((2, BLK, width), F32)],
        8,
    )(parity, *[came[r] for r in order], *[sibs[r] for r in order], sib, base, tokens, cotangent, gain)


def per_device(tokens, gain, w_qkv, w_out, nbr_list, nbr_count, cotangent):
    devices = lax.axis_size("seq")
    chips = devices // 2
    count, width = tokens.shape
    blocks = count // BLK
    plan, fetch_order, give_order = exchange_rounds(chips)
    rounds = len(plan)
    mate = [(i, i ^ 1) for i in range(devices)]

    def send(x, pairs):
        return lax.ppermute(x, "seq", [(2 * s + c, 2 * r + c) for r, s in pairs for c in range(2)])

    arrived, passed = [None] * rounds, [None] * rounds
    for r in fetch_order:
        source = plan[r].source
        arrived[r] = send(tokens if source is None else arrived[source], plan[r].fetch)
    for r in fetch_order:
        passed[r] = lax.ppermute(arrived[r], "seq", mate)
    direct = [r for r in fetch_order if plan[r].source is None]
    relayed = [r for r in fetch_order if plan[r].source is not None]
    windows, places = [tokens], [0]
    for some in (direct, relayed):
        windows += [arrived[r] for r in some]
        places += [2 * (r + 1) for r in some]
        if some is direct:
            windows.append(lax.ppermute(tokens, "seq", mate))
            places.append(1)
        windows += [passed[r] for r in some]
        places += [2 * (r + 1) + 1 for r in some]

    position = lax.axis_index("seq")
    chip, core = position // 2, position % 2
    my_lists = lax.dynamic_slice_in_dim(nbr_list, position * blocks, blocks, 0)
    my_counts = lax.dynamic_slice_in_dim(nbr_count, position * blocks, blocks, 0)
    owner = my_lists // blocks
    block = my_lists % blocks
    turn = round_of(chips, chip, owner // 2)
    other = (owner % 2) ^ core
    source = (turn * 2 + other) * 2 + block
    target = jnp.where(owner == position, block, 1 + 2 * turn + other)
    live = jnp.arange(MAXNB)[None, :] < my_counts[:, None]
    target = jnp.where(live, target, 3 + 2 * rounds)
    named = jnp.any(source.reshape(-1, 1) == jnp.arange(4 * (rounds + 1))[None, :], axis=0)
    meta = jnp.concatenate([source.reshape(-1), target.reshape(-1), my_counts, named]).astype(jnp.int32)

    all_live = jnp.arange(MAXNB)[None, :] < nbr_count[:, None]
    names_odd = jnp.any((all_live & (nbr_list == position * blocks + 1)).reshape(devices, -1), axis=1)
    givers = jnp.stack([position ^ 1] + [plan[r].giver(chip) * 2 + core for r in range(rounds)]
                       + [plan[r].giver(chip) * 2 + (1 - core) for r in range(rounds)])
    parity = jnp.take(names_odd.astype(jnp.int32), jnp.clip(givers, 0, devices - 1))

    gain = gain.reshape(1, width)
    unit, _ = layer_norm(tokens.astype(F32))
    normed = (unit * gain).astype(BF16)
    queries = jnp.dot(normed, w_qkv[:, :width], preferred_element_type=F32).astype(BF16)
    out_grad = dot(cotangent, w_out, 1, 1).astype(BF16)
    attended, query_grad, own, sib, *messages = main_call(meta, places, windows, queries, out_grad, gain, w_qkv)

    came, sibs = [None] * rounds, [None] * rounds
    first, last = give_order[0], give_order[-1]
    for r in give_order:
        if r == last:
            layer_out, base = middle_call(
                1 + first, parity, came[first], attended, query_grad, own, tokens, w_qkv, w_out
            )
            messages[r], layer_out, base = lax.optimization_barrier((messages[r], layer_out, base))
        came[r] = send(messages[r], plan[r].give)
    came[first], sib = lax.optimization_barrier((came[first], sib))
    sib = lax.ppermute(sib, "seq", mate)
    for r in give_order:
        sibs[r] = lax.ppermute(came[r], "seq", mate)
    token_grad = final_call(give_order, first, parity, came, sibs, sib, base, tokens, cotangent, gain)
    return (layer_out, token_grad)


def solution(mesh):
    in_specs = (
        P(("groups", "seq"), None),
        P(),
        P(),
        P(),
        P("groups", None),
        P("groups"),
        P(("groups", "seq"), None),
    )
    out_specs = (P(("groups", "seq"), None), P(("groups", "seq"), None))
    return jax.shard_map(
        per_device, mesh=mesh, in_specs=in_specs, out_specs=out_specs, check_vma=False
    )
```

```python
import functools

import jax
import jax.numpy as jnp
from jax import lax
from jax.experimental import pallas as pl
from jax.experimental.pallas import tpu as pltpu
from jax.sharding import PartitionSpec as P

HD = 64
BLK = 64
MAXNB = 8
HALF = 8
PACK = 4
REACH = (HALF + 1) // 2
F32 = jnp.float32
BF16 = jnp.bfloat16


class Round:
    def __init__(self, fetch, source, give, giver):
        self.fetch, self.source, self.give, self.giver = fetch, source, give, giver


def exchange_rounds(chips):
    near = lambda a, b: 0 <= a < chips and 0 <= b < chips and abs(a - b) <= REACH
    if chips == 8:
        rounds = []
        for m in range(1, 8):
            pairs = [(k, k ^ m) for k in range(chips) if near(k, k ^ m)]
            relay = m in (3, 5, 7)
            fetch = [(k, k ^ 1) for k, _ in pairs] if relay else pairs
            rounds.append(Round(fetch, (m ^ 1) - 1 if relay else None, pairs, lambda k, m=m: k ^ m))
        return rounds, [5, 0, 3, 1, 2, 6, 4], [3, 1, 0, 4, 2, 5, 6], 0
    rounds = []
    for d in range(-REACH, REACH + 1):
        if d != 0:
            pairs = [(k, k + d) for k in range(chips) if near(k, k + d)]
            rounds.append(Round(pairs, None, [(s, r) for r, s in pairs], lambda k, d=d: k - d))
    return rounds, list(range(len(rounds))), list(range(len(rounds))), 0


def round_of(chips, mine, peer):
    if chips == 8:
        return mine ^ peer
    d = peer - mine
    return jnp.where(d < 0, d + REACH + 1, jnp.where(d == 0, 0, d + REACH))


def layer_norm(x):
    center = jnp.mean(x, axis=-1, keepdims=True)
    spread = jnp.mean((x - center) ** 2, axis=-1, keepdims=True)
    inv_std = lax.rsqrt(spread + 1e-05)
    return (x - center) * inv_std, inv_std


def dot(a, b, ca, cb):
    return lax.dot_general(a, b, (((ca,), (cb,)), ((), ())), preferred_element_type=F32)


def call(kernel, out_shape, in_specs, out_specs, scratch, mib, flops=0):
    return pl.pallas_call(
        kernel,
        out_shape=out_shape,
        in_specs=in_specs,
        out_specs=out_specs,
        scratch_shapes=scratch,
        compiler_params=pltpu.CompilerParams(vmem_limit_bytes=mib * 2**20),
        cost_estimate=pl.CostEstimate(flops=flops, bytes_accessed=5 * 10**6, transcendentals=0),
    )


SMEM = pl.BlockSpec(memory_space=pltpu.SMEM)
VMEM = pl.BlockSpec(memory_space=pltpu.VMEM)
HBM = pl.BlockSpec(memory_space=pltpu.HBM)


def weight_copies(source, target, sems, from_column):
    rows, columns = target.shape
    band = rows // sems.shape[0]
    return [
        pltpu.make_async_copy(
            source.at[pl.ds(i * band, band), pl.ds(from_column, columns)],
            target.at[pl.ds(i * band, band)],
            sems.at[i],
        )
        for i in range(sems.shape[0])
    ]


def main_kernel(rounds, places, chips, position, lists, counts, *refs):
    count = len(places)
    windows = refs[:count]
    q_ref, g_ref, gain_ref, w_hbm = refs[count : count + 4]
    att_ref, dq_ref, own_ref, sib_ref = refs[count + 4 : count + 8]
    msg_refs = refs[count + 8 : count + 8 + rounds]
    xs, normed, kv, kvt, acc, w, source, target, named, wsems = refs[count + 8 + rounds :]
    width = q_ref.shape[1]
    wcopies = weight_copies(w_hbm, w, wsems, w_hbm.shape[1] - 2 * width)
    for c in wcopies:
        c.start()
    slots = 2 * MAXNB
    span = MAXNB * BLK

    me = position[0]
    for i in range(2 * count):
        named[i] = 0
    for s in range(slots):
        b, j = s // MAXNB, s % MAXNB
        block = lists[(2 * me + b) * MAXNB + j]
        owner = lax.shift_right_logical(block, 1)
        turn = round_of(chips, lax.shift_right_logical(me, 1), lax.shift_right_logical(owner, 1))
        place = 2 * turn + ((owner ^ me) & 1)
        found = 2 * place + (block & 1)
        source[s] = found
        named[found] = 1
        goal = jnp.where(place == 0, block & 1, 1 + place)
        target[s] = jnp.where(j < counts[2 * me + b], goal, 3 + 2 * rounds)

    gain = gain_ref[...]
    for ref, place in zip(windows, places):
        for j in range(2):

            @pl.when(named[2 * place + j] != 0)
            def _():
                xs[2 * place + j] = ref[j * BLK : (j + 1) * BLK, :]

    @pl.loop(0, slots, unroll=4)
    def _(s):
        unit, _ = layer_norm(xs[source[s]].astype(F32))
        normed[pl.ds(pl.multiple_of(s * BLK, BLK), BLK), :] = (unit * gain).astype(BF16)

    for c in wcopies:
        c.wait()
    rows = 256
    for i in range(slots * BLK // rows):
        kv[pl.ds(i * rows, rows), :] = dot(normed[pl.ds(i * rows, rows), :], w[...], 1, 0).astype(BF16)
    acc[...] = jnp.zeros_like(acc)

    group = PACK * HD
    lane = lax.broadcasted_iota(jnp.int32, (1, group), 1)
    masks = [(lane // HD == h).astype(BF16) for h in range(PACK)]
    slot_row = lax.broadcasted_iota(jnp.int32, (span, 1), 0)

    def diagonal(x):
        out = x[:BLK]
        for h in range(1, PACK):
            out = jnp.where(lane < h * HD, out, x[h * BLK : (h + 1) * BLK])
        return out

    for b in range(2):
        live = slot_row < counts[2 * me + b] * BLK
        for p in range(width // group):
            lanes = pl.ds(p * group, group)
            vlanes = pl.ds(width + p * group, group)
            tok = pl.ds(b * BLK, BLK)
            krows = pl.ds(b * span, span)
            q = q_ref[tok, lanes] * 0.125
            g = g_ref[tok, lanes]
            qd = jnp.concatenate([q * m for m in masks], axis=0)
            gd = jnp.concatenate([g * m for m in masks], axis=0)
            k = kv[krows, lanes]
            v = kv[krows, vlanes]
            scores = jnp.where(live, dot(k, qd, 1, 1), -1e30)
            weights = jnp.exp(scores - jnp.max(scores, axis=0, keepdims=True))
            pg = dot(v, gd, 1, 1)
            inverse = 1.0 / jnp.sum(weights, axis=0, keepdims=True)
            row_dot = jnp.sum(weights * pg, axis=0, keepdims=True) * inverse
            prob = weights * inverse
            low_prob = prob.astype(BF16)
            sg = (prob * (pg - row_dot)).astype(BF16)
            kvt[krows, lanes] = dot(sg, qd, 1, 0).astype(BF16)
            kvt[krows, vlanes] = dot(low_prob, gd, 1, 0).astype(BF16)
            att_ref[tok, lanes] = diagonal(dot(low_prob, v, 0, 0)).astype(BF16)
            dq_ref[tok, lanes] = (diagonal(dot(sg, k, 0, 0)) * 0.125).astype(BF16)

    for i in range(slots * BLK // rows):
        part = dot(kvt[pl.ds(i * rows, rows), :], w[...], 1, 1)
        for j in range(rows // BLK):
            at = target[i * (rows // BLK) + j]
            acc[at] = acc[at] + part[j * BLK : (j + 1) * BLK, :]
    for r in range(rounds):
        msg_refs[r][0:BLK, :] = acc[3 + 2 * r].astype(BF16)
        msg_refs[r][BLK : 2 * BLK, :] = acc[4 + 2 * r].astype(BF16)
    own_ref[0:BLK, :] = acc[0]
    own_ref[BLK : 2 * BLK, :] = acc[1]
    sib_ref[...] = acc[2].astype(BF16)


def main_call(chips, position, lists, counts, places, windows, queries, grads, gain, w_qkv):
    rounds = len(windows) // 2 - 1
    tokens, width = queries.shape
    slots = 2 * MAXNB
    shape = jax.ShapeDtypeStruct
    return call(
        functools.partial(main_kernel, rounds, places, chips),
        [shape((tokens, width), BF16)] * 2
        + [shape((tokens, width), F32), shape((BLK, width), BF16)]
        + [shape((2 * BLK, width), BF16)] * rounds,
        [SMEM] * 3 + [VMEM] * (len(windows) + 3) + [HBM],
        [VMEM] * (4 + rounds),
        [
            pltpu.VMEM((2 * len(windows), BLK, width), BF16),
            pltpu.VMEM((slots * BLK, width), BF16),
            pltpu.VMEM((slots * BLK, 2 * width), BF16),
            pltpu.VMEM((slots * BLK, 2 * width), BF16),
            pltpu.VMEM((4 + 2 * rounds, BLK, width), F32),
            pltpu.VMEM((width, 2 * width), BF16),
            pltpu.SMEM((slots,), jnp.int32),
            pltpu.SMEM((slots,), jnp.int32),
            pltpu.SMEM((2 * len(windows),), jnp.int32),
            pltpu.SemaphoreType.DMA((6,)),
        ],
        48,
        8 * 10**9,
    )(position, lists, counts, *windows, queries, grads, gain, w_qkv)


def add_came(total, came, at, rows):
    total[at] = total[at] + came[rows, :].astype(F32)


def middle_kernel(rows_of, parity, came, *refs):
    att_ref, dq_ref, own_ref, tok_ref, wqkv_hbm, wout_hbm, out_ref, total, wq, wout, qsems, osems = refs
    copies = weight_copies(wout_hbm, wout, osems, 0)
    q_copies = weight_copies(wqkv_hbm, wq, qsems, 0)
    for c in copies + q_copies:
        c.start()
    for c in copies:
        c.wait()
    out = tok_ref[...].astype(F32) + dot(att_ref[...], wout[...], 1, 0)
    out_ref[...] = out.astype(BF16)
    for c in q_copies:
        c.wait()
    base = own_ref[...] + dot(dq_ref[...], wq[...], 1, 1)
    for b in range(2):
        total[b] = base[b * BLK : (b + 1) * BLK, :]
    add_came(total, came, parity[rows_of], pl.ds(0, BLK))


def middle_call(rows_of, parity, came, attended, query_grad, own, tokens, w_qkv, w_out):
    count, width = tokens.shape
    return call(
        functools.partial(middle_kernel, rows_of),
        [jax.ShapeDtypeStruct((count, width), BF16), jax.ShapeDtypeStruct((2, BLK, width), F32)],
        [SMEM] + [VMEM] * 5 + [HBM] * 2,
        [VMEM] * 2,
        [pltpu.VMEM((width, width), BF16)] * 2 + [pltpu.SemaphoreType.DMA((4,))] * 2,
        48,
    )(parity, came, attended, query_grad, own, tokens, w_qkv, w_out)


def final_kernel(order, done, parity, *refs):
    rounds = len(order)
    came, sibs = dict(zip(order, refs[:rounds])), dict(zip(order, refs[rounds : 2 * rounds]))
    sib, base, tok_ref, cot_ref, gain_ref, out_ref, total = refs[2 * rounds :]
    total[...] = base[...]
    add_came(total, sib, parity[0], pl.ds(0, BLK))
    for r in range(rounds):
        if r != done:
            add_came(total, came[r], parity[1 + r], pl.ds(0, BLK))
        add_came(total, sibs[r], parity[1 + rounds + r], pl.ds(BLK, BLK))
    gain = gain_ref[...]
    for b in range(2):
        rows = pl.ds(b * BLK, BLK)
        unit, inv_std = layer_norm(tok_ref[rows, :].astype(F32))
        scaled = total[b] * gain
        centered = (
            scaled
            - jnp.mean(scaled, axis=-1, keepdims=True)
            - unit * jnp.mean(scaled * unit, axis=-1, keepdims=True)
        )
        out_ref[rows, :] = (cot_ref[rows, :].astype(F32) + inv_std * centered).astype(BF16)


def final_call(order, done, parity, came, sibs, sib, base, tokens, cotangent, gain):
    rounds = len(came)
    count, width = tokens.shape
    return call(
        functools.partial(final_kernel, order, done),
        jax.ShapeDtypeStruct((count, width), BF16),
        [SMEM] + [VMEM] * (2 * rounds + 5),
        VMEM,
        [pltpu.VMEM((2, BLK, width), F32)],
        8,
    )(parity, *[came[r] for r in order], *[sibs[r] for r in order], sib, base, tokens, cotangent, gain)


def per_device(tokens, gain, w_qkv, w_out, nbr_list, nbr_count, cotangent):
    devices = lax.axis_size("seq")
    chips = devices // 2
    count, width = tokens.shape
    blocks = count // BLK
    plan, fetch_order, give_order, early = exchange_rounds(chips)
    rounds = len(plan)
    mate = [(i, i ^ 1) for i in range(devices)]

    def send(x, pairs):
        return lax.ppermute(x, "seq", [(2 * s + c, 2 * r + c) for r, s in pairs for c in range(2)])

    arrived, passed = [None] * rounds, [None] * rounds
    for r in fetch_order:
        source = plan[r].source
        arrived[r] = send(tokens if source is None else arrived[source], plan[r].fetch)
    position = lax.axis_index("seq")
    live = jnp.arange(MAXNB)[None, :] < nbr_count[:, None]
    names_odd = jnp.any(live & (nbr_list == position * blocks + 1), axis=1)
    givers = jnp.stack([position ^ 1] + [
        plan[r].giver(position // 2) * 2 + ((position % 2) ^ other) for other in range(2) for r in range(rounds)
    ])
    row_owner = jnp.arange(nbr_list.shape[0]) // blocks
    parity = jnp.any(names_odd[None, :] & (row_owner[None, :] == givers[:, None]), axis=1).astype(jnp.int32)

    gain = gain.reshape(1, width)
    lists = nbr_list.reshape(-1)
    unit, _ = layer_norm(tokens.astype(F32))
    normed = (unit * gain).astype(BF16)
    queries = jnp.dot(normed, w_qkv[:, :width], preferred_element_type=F32).astype(BF16)
    out_grad = dot(cotangent, w_out, 1, 1).astype(BF16)
    arrived[early], parity, lists, gain = lax.optimization_barrier(
        (arrived[early], parity, lists, gain)
    )
    for r in fetch_order:
        passed[r] = lax.ppermute(arrived[r], "seq", mate)
    direct = [r for r in fetch_order if plan[r].source is None]
    relayed = [r for r in fetch_order if plan[r].source is not None]
    windows, places = [tokens], [0]
    for some in (direct, relayed):
        windows += [arrived[r] for r in some]
        places += [2 * (r + 1) for r in some]
        if some is direct:
            windows.append(lax.ppermute(tokens, "seq", mate))
            places.append(1)
        windows += [passed[r] for r in some]
        places += [2 * (r + 1) + 1 for r in some]

    attended, query_grad, own, sib, *messages = main_call(
        chips, position.reshape(1), lists, nbr_count, places, windows, queries, out_grad, gain, w_qkv
    )

    came, sibs = [None] * rounds, [None] * rounds
    first, last = give_order[0], give_order[-1]
    for r in give_order:
        if r == last:
            layer_out, base = middle_call(
                1 + first, parity, came[first], attended, query_grad, own, tokens, w_qkv, w_out
            )
            messages[r], layer_out, base = lax.optimization_barrier((messages[r], layer_out, base))
        came[r] = send(messages[r], plan[r].give)
    came[first], sib = lax.optimization_barrier((came[first], sib))
    sib = lax.ppermute(sib, "seq", mate)
    for r in give_order:
        sibs[r] = lax.ppermute(came[r], "seq", mate)
    token_grad = final_call(give_order, first, parity, came, sibs, sib, base, tokens, cotangent, gain)
    return (layer_out, token_grad)


def solution(mesh):
    in_specs = (
        P(("groups", "seq"), None),
        P(),
        P(),
        P(),
        P("groups", None),
        P("groups"),
        P(("groups", "seq"), None),
    )
    out_specs = (P(("groups", "seq"), None), P(("groups", "seq"), None))
    return jax.shard_map(
        per_device, mesh=mesh, in_specs=in_specs, out_specs=out_specs, check_vma=False
    )
```

```python
import functools

import jax
import jax.numpy as jnp
from jax import lax
from jax.experimental import pallas as pl
from jax.experimental.pallas import tpu as pltpu
from jax.sharding import PartitionSpec as P

HD = 64
BLK = 64
MAXNB = 8
HALF = 8
PACK = 4
REACH = (HALF + 1) // 2
F32 = jnp.float32
BF16 = jnp.bfloat16


class Round:
    def __init__(self, fetch, source, give, giver):
        self.fetch, self.source, self.give, self.giver = fetch, source, give, giver


def exchange_rounds(chips):
    near = lambda a, b: 0 <= a < chips and 0 <= b < chips and abs(a - b) <= REACH
    if chips == 8:
        rounds = []
        for m in range(1, 8):
            pairs = [(k, k ^ m) for k in range(chips) if near(k, k ^ m)]
            relay = m in (5, 7)
            fetch = [(k, k ^ 1) for k, _ in pairs] if relay else pairs
            rounds.append(Round(fetch, (m ^ 1) - 1 if relay else None, pairs, lambda k, m=m: k ^ m))
        return rounds, [1, 5, 2, 0, 3, 4, 6], [3, 1, 0, 4, 2, 5, 6], 0
    rounds = []
    for d in range(-REACH, REACH + 1):
        if d != 0:
            pairs = [(k, k + d) for k in range(chips) if near(k, k + d)]
            rounds.append(Round(pairs, None, [(s, r) for r, s in pairs], lambda k, d=d: k - d))
    return rounds, list(range(len(rounds))), list(range(len(rounds))), 0


def round_of(chips, mine, peer):
    if chips == 8:
        return mine ^ peer
    d = peer - mine
    return jnp.where(d < 0, d + REACH + 1, jnp.where(d == 0, 0, d + REACH))


def layer_norm(x):
    center = jnp.mean(x, axis=-1, keepdims=True)
    spread = jnp.mean((x - center) ** 2, axis=-1, keepdims=True)
    inv_std = lax.rsqrt(spread + 1e-05)
    return (x - center) * inv_std, inv_std


def dot(a, b, ca, cb):
    return lax.dot_general(a, b, (((ca,), (cb,)), ((), ())), preferred_element_type=F32)


def call(kernel, out_shape, in_specs, out_specs, scratch, mib, flops=0):
    return pl.pallas_call(
        kernel,
        out_shape=out_shape,
        in_specs=in_specs,
        out_specs=out_specs,
        scratch_shapes=scratch,
        compiler_params=pltpu.CompilerParams(vmem_limit_bytes=mib * 2**20),
        cost_estimate=pl.CostEstimate(flops=flops, bytes_accessed=5 * 10**6, transcendentals=0),
    )


SMEM = pl.BlockSpec(memory_space=pltpu.SMEM)
VMEM = pl.BlockSpec(memory_space=pltpu.VMEM)
HBM = pl.BlockSpec(memory_space=pltpu.HBM)


def weight_copies(source, target, sems, from_column):
    rows, columns = target.shape
    band = rows // sems.shape[0]
    return [
        pltpu.make_async_copy(
            source.at[pl.ds(i * band, band), pl.ds(from_column, columns)],
            target.at[pl.ds(i * band, band)],
            sems.at[i],
        )
        for i in range(sems.shape[0])
    ]


def main_kernel(rounds, places, chips, position, lists, counts, *refs):
    count = len(places)
    windows = refs[:count]
    q_ref, g_ref, gain_ref, w_hbm = refs[count : count + 4]
    att_ref, dq_ref, own_ref, sib_ref = refs[count + 4 : count + 8]
    msg_refs = refs[count + 8 : count + 8 + rounds]
    xs, normed, kv, kvt, acc, w, source, target, named, wsems = refs[count + 8 + rounds :]
    width = q_ref.shape[1]
    wcopies = weight_copies(w_hbm, w, wsems, w_hbm.shape[1] - 2 * width)
    for c in wcopies:
        c.start()
    slots = 2 * MAXNB
    span = MAXNB * BLK

    me = position[0]
    for i in range(2 * count):
        named[i] = 0
    for s in range(slots):
        b, j = s // MAXNB, s % MAXNB
        block = lists[(2 * me + b) * MAXNB + j]
        owner = lax.shift_right_logical(block, 1)
        turn = round_of(chips, lax.shift_right_logical(me, 1), lax.shift_right_logical(owner, 1))
        place = 2 * turn + ((owner ^ me) & 1)
        found = 2 * place + (block & 1)
        source[s] = found
        named[found] = 1
        goal = jnp.where(place == 0, block & 1, 1 + place)
        target[s] = jnp.where(j < counts[2 * me + b], goal, 3 + 2 * rounds)

    gain = gain_ref[...]
    for ref, place in zip(windows, places):
        for j in range(2):

            @pl.when(named[2 * place + j] != 0)
            def _():
                xs[2 * place + j] = ref[j * BLK : (j + 1) * BLK, :]

    @pl.loop(0, slots, unroll=4)
    def _(s):
        unit, _ = layer_norm(xs[source[s]].astype(F32))
        normed[pl.ds(pl.multiple_of(s * BLK, BLK), BLK), :] = (unit * gain).astype(BF16)

    for c in wcopies:
        c.wait()
    rows = 256
    for i in range(slots * BLK // rows):
        kv[pl.ds(i * rows, rows), :] = dot(normed[pl.ds(i * rows, rows), :], w[...], 1, 0).astype(BF16)
    acc[...] = jnp.zeros_like(acc)

    group = PACK * HD
    lane = lax.broadcasted_iota(jnp.int32, (1, group), 1)
    masks = [(lane // HD == h).astype(BF16) for h in range(PACK)]
    slot_row = lax.broadcasted_iota(jnp.int32, (span, 1), 0)

    def diagonal(x):
        out = x[:BLK]
        for h in range(1, PACK):
            out = jnp.where(lane < h * HD, out, x[h * BLK : (h + 1) * BLK])
        return out

    for b in range(2):
        live = slot_row < counts[2 * me + b] * BLK
        for p in range(width // group):
            lanes = pl.ds(p * group, group)
            vlanes = pl.ds(width + p * group, group)
            tok = pl.ds(b * BLK, BLK)
            krows = pl.ds(b * span, span)
            q = q_ref[tok, lanes] * 0.125
            g = g_ref[tok, lanes]
            qd = jnp.concatenate([q * m for m in masks], axis=0)
            gd = jnp.concatenate([g * m for m in masks], axis=0)
            k = kv[krows, lanes]
            v = kv[krows, vlanes]
            scores = jnp.where(live, dot(k, qd, 1, 1), -1e30)
            weights = jnp.exp(scores - jnp.max(scores, axis=0, keepdims=True))
            pg = dot(v, gd, 1, 1)
            inverse = 1.0 / jnp.sum(weights, axis=0, keepdims=True)
            row_dot = jnp.sum(weights * pg, axis=0, keepdims=True) * inverse
            prob = weights * inverse
            low_prob = prob.astype(BF16)
            sg = (prob * (pg - row_dot)).astype(BF16)
            kvt[krows, lanes] = dot(sg, qd, 1, 0).astype(BF16)
            kvt[krows, vlanes] = dot(low_prob, gd, 1, 0).astype(BF16)
            att_ref[tok, lanes] = diagonal(dot(low_prob, v, 0, 0)).astype(BF16)
            dq_ref[tok, lanes] = (diagonal(dot(sg, k, 0, 0)) * 0.125).astype(BF16)

    for i in range(slots * BLK // rows):
        part = dot(kvt[pl.ds(i * rows, rows), :], w[...], 1, 1)
        for j in range(rows // BLK):
            at = target[i * (rows // BLK) + j]
            acc[at] = acc[at] + part[j * BLK : (j + 1) * BLK, :]
    for r in range(rounds):
        msg_refs[r][0:BLK, :] = acc[3 + 2 * r].astype(BF16)
        msg_refs[r][BLK : 2 * BLK, :] = acc[4 + 2 * r].astype(BF16)
    own_ref[0:BLK, :] = acc[0]
    own_ref[BLK : 2 * BLK, :] = acc[1]
    sib_ref[...] = acc[2].astype(BF16)


def main_call(chips, position, lists, counts, places, windows, queries, grads, gain, w_qkv):
    rounds = len(windows) // 2 - 1
    tokens, width = queries.shape
    slots = 2 * MAXNB
    shape = jax.ShapeDtypeStruct
    return call(
        functools.partial(main_kernel, rounds, places, chips),
        [shape((tokens, width), BF16)] * 2
        + [shape((tokens, width), F32), shape((BLK, width), BF16)]
        + [shape((2 * BLK, width), BF16)] * rounds,
        [SMEM] * 3 + [VMEM] * (len(windows) + 3) + [HBM],
        [VMEM] * (4 + rounds),
        [
            pltpu.VMEM((2 * len(windows), BLK, width), BF16),
            pltpu.VMEM((slots * BLK, width), BF16),
            pltpu.VMEM((slots * BLK, 2 * width), BF16),
            pltpu.VMEM((slots * BLK, 2 * width), BF16),
            pltpu.VMEM((4 + 2 * rounds, BLK, width), F32),
            pltpu.VMEM((width, 2 * width), BF16),
            pltpu.SMEM((slots,), jnp.int32),
            pltpu.SMEM((slots,), jnp.int32),
            pltpu.SMEM((2 * len(windows),), jnp.int32),
            pltpu.SemaphoreType.DMA((6,)),
        ],
        48,
        8 * 10**9,
    )(position, lists, counts, *windows, queries, grads, gain, w_qkv)


def add_came(total, came, at, rows):
    total[at] = total[at] + came[rows, :].astype(F32)


def middle_kernel(rows_of, parity, came, *refs):
    att_ref, dq_ref, own_ref, tok_ref, wqkv_hbm, wout_hbm, out_ref, total, wq, wout, qsems, osems = refs
    copies = weight_copies(wout_hbm, wout, osems, 0)
    q_copies = weight_copies(wqkv_hbm, wq, qsems, 0)
    for c in copies + q_copies:
        c.start()
    for c in copies:
        c.wait()
    out = tok_ref[...].astype(F32) + dot(att_ref[...], wout[...], 1, 0)
    out_ref[...] = out.astype(BF16)
    for c in q_copies:
        c.wait()
    base = own_ref[...] + dot(dq_ref[...], wq[...], 1, 1)
    for b in range(2):
        total[b] = base[b * BLK : (b + 1) * BLK, :]
    add_came(total, came, parity[rows_of], pl.ds(0, BLK))


def middle_call(rows_of, parity, came, attended, query_grad, own, tokens, w_qkv, w_out):
    count, width = tokens.shape
    return call(
        functools.partial(middle_kernel, rows_of),
        [jax.ShapeDtypeStruct((count, width), BF16), jax.ShapeDtypeStruct((2, BLK, width), F32)],
        [SMEM] + [VMEM] * 5 + [HBM] * 2,
        [VMEM] * 2,
        [pltpu.VMEM((width, width), BF16)] * 2 + [pltpu.SemaphoreType.DMA((4,))] * 2,
        48,
    )(parity, came, attended, query_grad, own, tokens, w_qkv, w_out)


def final_kernel(order, done, parity, *refs):
    rounds = len(order)
    came, sibs = dict(zip(order, refs[:rounds])), dict(zip(order, refs[rounds : 2 * rounds]))
    sib, base, tok_ref, cot_ref, gain_ref, out_ref, total = refs[2 * rounds :]
    total[...] = base[...]
    add_came(total, sib, parity[0], pl.ds(0, BLK))
    for r in range(rounds):
        if r != done:
            add_came(total, came[r], parity[1 + r], pl.ds(0, BLK))
        add_came(total, sibs[r], parity[1 + rounds + r], pl.ds(BLK, BLK))
    gain = gain_ref[...]
    for b in range(2):
        rows = pl.ds(b * BLK, BLK)
        unit, inv_std = layer_norm(tok_ref[rows, :].astype(F32))
        scaled = total[b] * gain
        centered = (
            scaled
            - jnp.mean(scaled, axis=-1, keepdims=True)
            - unit * jnp.mean(scaled * unit, axis=-1, keepdims=True)
        )
        out_ref[rows, :] = (cot_ref[rows, :].astype(F32) + inv_std * centered).astype(BF16)


def final_call(order, done, parity, came, sibs, sib, base, tokens, cotangent, gain):
    rounds = len(came)
    count, width = tokens.shape
    return call(
        functools.partial(final_kernel, order, done),
        jax.ShapeDtypeStruct((count, width), BF16),
        [SMEM] + [VMEM] * (2 * rounds + 5),
        VMEM,
        [pltpu.VMEM((2, BLK, width), F32)],
        8,
    )(parity, *[came[r] for r in order], *[sibs[r] for r in order], sib, base, tokens, cotangent, gain)


def per_device(tokens, gain, w_qkv, w_out, nbr_list, nbr_count, cotangent):
    devices = lax.axis_size("seq")
    chips = devices // 2
    count, width = tokens.shape
    blocks = count // BLK
    plan, fetch_order, give_order, early = exchange_rounds(chips)
    rounds = len(plan)
    mate = [(i, i ^ 1) for i in range(devices)]

    def send(x, pairs):
        return lax.ppermute(x, "seq", [(2 * s + c, 2 * r + c) for r, s in pairs for c in range(2)])

    arrived, passed = [None] * rounds, [None] * rounds
    for r in fetch_order:
        source = plan[r].source
        arrived[r] = send(tokens if source is None else arrived[source], plan[r].fetch)
    position = lax.axis_index("seq")
    live = jnp.arange(MAXNB)[None, :] < nbr_count[:, None]
    names_odd = jnp.any(live & (nbr_list == position * blocks + 1), axis=1)
    givers = jnp.stack([position ^ 1] + [
        plan[r].giver(position // 2) * 2 + ((position % 2) ^ other) for other in range(2) for r in range(rounds)
    ])
    row_owner = jnp.arange(nbr_list.shape[0]) // blocks
    parity = jnp.any(names_odd[None, :] & (row_owner[None, :] == givers[:, None]), axis=1).astype(jnp.int32)

    gain = gain.reshape(1, width)
    lists = nbr_list.reshape(-1)
    unit, _ = layer_norm(tokens.astype(F32))
    normed = (unit * gain).astype(BF16)
    queries = jnp.dot(normed, w_qkv[:, :width], preferred_element_type=F32).astype(BF16)
    out_grad = dot(cotangent, w_out, 1, 1).astype(BF16)
    arrived[early], parity, lists, gain = lax.optimization_barrier(
        (arrived[early], parity, lists, gain)
    )
    for r in fetch_order:
        passed[r] = lax.ppermute(arrived[r], "seq", mate)
    direct = [r for r in fetch_order if plan[r].source is None]
    relayed = [r for r in fetch_order if plan[r].source is not None]
    windows, places = [tokens], [0]
    for some in (direct, relayed):
        windows += [arrived[r] for r in some]
        places += [2 * (r + 1) for r in some]
        if some is direct:
            windows.append(lax.ppermute(tokens, "seq", mate))
            places.append(1)
        windows += [passed[r] for r in some]
        places += [2 * (r + 1) + 1 for r in some]

    attended, query_grad, own, sib, *messages = main_call(
        chips, position.reshape(1), lists, nbr_count, places, windows, queries, out_grad, gain, w_qkv
    )

    came, sibs = [None] * rounds, [None] * rounds
    first, last = give_order[0], give_order[-1]
    for r in give_order:
        if r == last:
            layer_out, base = middle_call(
                1 + first, parity, came[first], attended, query_grad, own, tokens, w_qkv, w_out
            )
            messages[r], layer_out, base = lax.optimization_barrier((messages[r], layer_out, base))
        came[r] = send(messages[r], plan[r].give)
    came[first], sib = lax.optimization_barrier((came[first], sib))
    sib = lax.ppermute(sib, "seq", mate)
    for r in give_order:
        sibs[r] = lax.ppermute(came[r], "seq", mate)
    token_grad = final_call(give_order, first, parity, came, sibs, sib, base, tokens, cotangent, gain)
    return (layer_out, token_grad)


def solution(mesh):
    in_specs = (
        P(("groups", "seq"), None),
        P(),
        P(),
        P(),
        P("groups", None),
        P("groups"),
        P(("groups", "seq"), None),
    )
    out_specs = (P(("groups", "seq"), None), P(("groups", "seq"), None))
    return jax.shard_map(
        per_device, mesh=mesh, in_specs=in_specs, out_specs=out_specs, check_vma=False
    )
```

```python
import functools

import jax
import jax.numpy as jnp
from jax import lax
from jax.experimental import pallas as pl
from jax.experimental.pallas import tpu as pltpu
from jax.sharding import PartitionSpec as P

HD = 64
BLK = 64
MAXNB = 8
HALF = 8
PACK = 4
REACH = (HALF + 1) // 2
F32 = jnp.float32
BF16 = jnp.bfloat16


class Round:
    def __init__(self, fetch, source, give, giver):
        self.fetch, self.source, self.give, self.giver = fetch, source, give, giver


def exchange_rounds(chips):
    near = lambda a, b: 0 <= a < chips and 0 <= b < chips and abs(a - b) <= REACH
    if chips == 8:
        rounds = []
        for m in range(1, 8):
            pairs = [(k, k ^ m) for k in range(chips) if near(k, k ^ m)]
            relay = m in (5, 7)
            fetch = [(k, k ^ 1) for k, _ in pairs] if relay else pairs
            rounds.append(Round(fetch, (m ^ 1) - 1 if relay else None, pairs, lambda k, m=m: k ^ m))
        return rounds, [1, 5, 2, 0, 3, 4, 6], [3, 1, 0, 4, 2, 5, 6], 0
    rounds = []
    for d in range(-REACH, REACH + 1):
        if d != 0:
            pairs = [(k, k + d) for k in range(chips) if near(k, k + d)]
            rounds.append(Round(pairs, None, [(s, r) for r, s in pairs], lambda k, d=d: k - d))
    return rounds, list(range(len(rounds))), list(range(len(rounds))), 0


def round_of(chips, mine, peer):
    if chips == 8:
        return mine ^ peer
    d = peer - mine
    return jnp.where(d < 0, d + REACH + 1, jnp.where(d == 0, 0, d + REACH))


def layer_norm(x):
    center = jnp.mean(x, axis=-1, keepdims=True)
    spread = jnp.mean((x - center) ** 2, axis=-1, keepdims=True)
    inv_std = lax.rsqrt(spread + 1e-05)
    return (x - center) * inv_std, inv_std


def dot(a, b, ca, cb):
    return lax.dot_general(a, b, (((ca,), (cb,)), ((), ())), preferred_element_type=F32)


def call(kernel, out_shape, in_specs, out_specs, scratch, mib, flops=0):
    return pl.pallas_call(
        kernel,
        out_shape=out_shape,
        in_specs=in_specs,
        out_specs=out_specs,
        scratch_shapes=scratch,
        compiler_params=pltpu.CompilerParams(vmem_limit_bytes=mib * 2**20),
        cost_estimate=pl.CostEstimate(flops=flops, bytes_accessed=5 * 10**6, transcendentals=0),
    )


SMEM = pl.BlockSpec(memory_space=pltpu.SMEM)
VMEM = pl.BlockSpec(memory_space=pltpu.VMEM)
HBM = pl.BlockSpec(memory_space=pltpu.HBM)


def weight_copies(source, target, sems, from_column):
    rows, columns = target.shape
    band = rows // sems.shape[0]
    return [
        pltpu.make_async_copy(
            source.at[pl.ds(i * band, band), pl.ds(from_column, columns)],
            target.at[pl.ds(i * band, band)],
            sems.at[i],
        )
        for i in range(sems.shape[0])
    ]


def main_kernel(rounds, places, chips, position, lists, counts, *refs):
    count = len(places)
    windows = refs[:count]
    q_ref, g_ref, gain_ref, w_hbm = refs[count : count + 4]
    att_ref, dq_ref, own_ref, sib_ref = refs[count + 4 : count + 8]
    msg_refs = refs[count + 8 : count + 8 + rounds]
    xs, normed, kv, kvt, acc, w, source, target, named, wsems = refs[count + 8 + rounds :]
    width = q_ref.shape[1]
    wcopies = weight_copies(w_hbm, w, wsems, w_hbm.shape[1] - 2 * width)
    for c in wcopies:
        c.start()
    acc[...] = jnp.zeros_like(acc)
    slots = 2 * MAXNB
    span = MAXNB * BLK

    me = position[0]
    for i in range(2 * count):
        named[i] = 0
    for s in range(slots):
        b, j = s // MAXNB, s % MAXNB
        block = lists[(2 * me + b) * MAXNB + j]
        owner = lax.shift_right_logical(block, 1)
        turn = round_of(chips, lax.shift_right_logical(me, 1), lax.shift_right_logical(owner, 1))
        place = 2 * turn + ((owner ^ me) & 1)
        found = 2 * place + (block & 1)
        source[s] = found
        named[found] = 1
        goal = jnp.where(place == 0, block & 1, 1 + place)
        target[s] = jnp.where(j < counts[2 * me + b], goal, 3 + 2 * rounds)

    gain = gain_ref[...]
    for ref, place in zip(windows, places):
        for j in range(2):

            @pl.when(named[2 * place + j] != 0)
            def _():
                xs[2 * place + j] = ref[j * BLK : (j + 1) * BLK, :]

    @pl.loop(0, slots, unroll=4)
    def _(s):
        unit, _ = layer_norm(xs[source[s]].astype(F32))
        normed[pl.ds(pl.multiple_of(s * BLK, BLK), BLK), :] = (unit * gain).astype(BF16)

    for c in wcopies:
        c.wait()
    rows = 256
    for i in range(slots * BLK // rows):
        kv[pl.ds(i * rows, rows), :] = dot(normed[pl.ds(i * rows, rows), :], w[...], 1, 0).astype(BF16)

    group = PACK * HD
    lane = lax.broadcasted_iota(jnp.int32, (1, group), 1)
    masks = [(lane // HD == h).astype(BF16) for h in range(PACK)]
    slot_row = lax.broadcasted_iota(jnp.int32, (span, 1), 0)

    def diagonal(x):
        out = x[:BLK]
        for h in range(1, PACK):
            out = jnp.where(lane < h * HD, out, x[h * BLK : (h + 1) * BLK])
        return out

    for b in range(2):
        live = slot_row < counts[2 * me + b] * BLK
        for p in range(width // group):
            lanes = pl.ds(p * group, group)
            vlanes = pl.ds(width + p * group, group)
            tok = pl.ds(b * BLK, BLK)
            krows = pl.ds(b * span, span)
            q = q_ref[tok, lanes] * 0.125
            g = g_ref[tok, lanes]
            qd = jnp.concatenate([q * m for m in masks], axis=0)
            gd = jnp.concatenate([g * m for m in masks], axis=0)
            k = kv[krows, lanes]
            v = kv[krows, vlanes]
            scores = jnp.where(live, dot(k, qd, 1, 1), -1e30)
            weights = jnp.exp(scores - jnp.max(scores, axis=0, keepdims=True))
            pg = dot(v, gd, 1, 1)
            inverse = 1.0 / jnp.sum(weights, axis=0, keepdims=True)
            row_dot = jnp.sum(weights * pg, axis=0, keepdims=True) * inverse
            prob = weights * inverse
            low_prob = prob.astype(BF16)
            sg = (prob * (pg - row_dot)).astype(BF16)
            kvt[krows, lanes] = dot(sg, qd, 1, 0).astype(BF16)
            kvt[krows, vlanes] = dot(low_prob, gd, 1, 0).astype(BF16)
            att_ref[tok, lanes] = diagonal(dot(low_prob, v, 0, 0)).astype(BF16)
            dq_ref[tok, lanes] = (diagonal(dot(sg, k, 0, 0)) * 0.125).astype(BF16)

    for i in range(slots * BLK // rows):
        part = dot(kvt[pl.ds(i * rows, rows), :], w[...], 1, 1)
        for j in range(rows // BLK):
            at = target[i * (rows // BLK) + j]
            acc[at] = acc[at] + part[j * BLK : (j + 1) * BLK, :]
    for r in range(rounds):
        msg_refs[r][0:BLK, :] = acc[3 + 2 * r].astype(BF16)
        msg_refs[r][BLK : 2 * BLK, :] = acc[4 + 2 * r].astype(BF16)
    own_ref[0:BLK, :] = acc[0]
    own_ref[BLK : 2 * BLK, :] = acc[1]
    sib_ref[...] = acc[2].astype(BF16)


def main_call(chips, position, lists, counts, places, windows, queries, grads, gain, w_qkv):
    rounds = len(windows) // 2 - 1
    tokens, width = queries.shape
    slots = 2 * MAXNB
    shape = jax.ShapeDtypeStruct
    return call(
        functools.partial(main_kernel, rounds, places, chips),
        [shape((tokens, width), BF16)] * 2
        + [shape((tokens, width), F32), shape((BLK, width), BF16)]
        + [shape((2 * BLK, width), BF16)] * rounds,
        [SMEM] * 3 + [VMEM] * (len(windows) + 3) + [HBM],
        [VMEM] * (4 + rounds),
        [
            pltpu.VMEM((2 * len(windows), BLK, width), BF16),
            pltpu.VMEM((slots * BLK, width), BF16),
            pltpu.VMEM((slots * BLK, 2 * width), BF16),
            pltpu.VMEM((slots * BLK, 2 * width), BF16),
            pltpu.VMEM((4 + 2 * rounds, BLK, width), F32),
            pltpu.VMEM((width, 2 * width), BF16),
            pltpu.SMEM((slots,), jnp.int32),
            pltpu.SMEM((slots,), jnp.int32),
            pltpu.SMEM((2 * len(windows),), jnp.int32),
            pltpu.SemaphoreType.DMA((6,)),
        ],
        48,
        8 * 10**9,
    )(position, lists, counts, *windows, queries, grads, gain, w_qkv)


def add_came(total, came, at, rows):
    total[at] = total[at] + came[rows, :].astype(F32)


def middle_kernel(rows_of, parity, came, *refs):
    att_ref, dq_ref, own_ref, tok_ref, wqkv_hbm, wout_hbm, out_ref, total, wq, wout, qsems, osems = refs
    copies = weight_copies(wout_hbm, wout, osems, 0)
    q_copies = weight_copies(wqkv_hbm, wq, qsems, 0)
    for c in copies + q_copies:
        c.start()
    for c in copies:
        c.wait()
    out = tok_ref[...].astype(F32) + dot(att_ref[...], wout[...], 1, 0)
    out_ref[...] = out.astype(BF16)
    for c in q_copies:
        c.wait()
    base = own_ref[...] + dot(dq_ref[...], wq[...], 1, 1)
    for b in range(2):
        total[b] = base[b * BLK : (b + 1) * BLK, :]
    add_came(total, came, parity[rows_of], pl.ds(0, BLK))


def middle_call(rows_of, parity, came, attended, query_grad, own, tokens, w_qkv, w_out):
    count, width = tokens.shape
    return call(
        functools.partial(middle_kernel, rows_of),
        [jax.ShapeDtypeStruct((count, width), BF16), jax.ShapeDtypeStruct((2, BLK, width), F32)],
        [SMEM] + [VMEM] * 5 + [HBM] * 2,
        [VMEM] * 2,
        [pltpu.VMEM((width, width), BF16)] * 2 + [pltpu.SemaphoreType.DMA((4,))] * 2,
        48,
    )(parity, came, attended, query_grad, own, tokens, w_qkv, w_out)


def final_kernel(order, done, parity, *refs):
    rounds = len(order)
    came, sibs = dict(zip(order, refs[:rounds])), dict(zip(order, refs[rounds : 2 * rounds]))
    sib, base, tok_ref, cot_ref, gain_ref, out_ref, total = refs[2 * rounds :]
    total[...] = base[...]
    add_came(total, sib, parity[0], pl.ds(0, BLK))
    for r in range(rounds):
        if r != done:
            add_came(total, came[r], parity[1 + r], pl.ds(0, BLK))
        add_came(total, sibs[r], parity[1 + rounds + r], pl.ds(BLK, BLK))
    gain = gain_ref[...]
    for b in range(2):
        rows = pl.ds(b * BLK, BLK)
        unit, inv_std = layer_norm(tok_ref[rows, :].astype(F32))
        scaled = total[b] * gain
        centered = (
            scaled
            - jnp.mean(scaled, axis=-1, keepdims=True)
            - unit * jnp.mean(scaled * unit, axis=-1, keepdims=True)
        )
        out_ref[rows, :] = (cot_ref[rows, :].astype(F32) + inv_std * centered).astype(BF16)


def final_call(order, done, parity, came, sibs, sib, base, tokens, cotangent, gain):
    rounds = len(came)
    count, width = tokens.shape
    return call(
        functools.partial(final_kernel, order, done),
        jax.ShapeDtypeStruct((count, width), BF16),
        [SMEM] + [VMEM] * (2 * rounds + 5),
        VMEM,
        [pltpu.VMEM((2, BLK, width), F32)],
        8,
    )(parity, *[came[r] for r in order], *[sibs[r] for r in order], sib, base, tokens, cotangent, gain)


def per_device(tokens, gain, w_qkv, w_out, nbr_list, nbr_count, cotangent):
    devices = lax.axis_size("seq")
    chips = devices // 2
    count, width = tokens.shape
    blocks = count // BLK
    plan, fetch_order, give_order, early = exchange_rounds(chips)
    rounds = len(plan)
    mate = [(i, i ^ 1) for i in range(devices)]

    def send(x, pairs):
        return lax.ppermute(x, "seq", [(2 * s + c, 2 * r + c) for r, s in pairs for c in range(2)])

    arrived, passed = [None] * rounds, [None] * rounds
    for r in fetch_order:
        source = plan[r].source
        arrived[r] = send(tokens if source is None else arrived[source], plan[r].fetch)
    position = lax.axis_index("seq")
    live = jnp.arange(MAXNB)[None, :] < nbr_count[:, None]
    names_odd = jnp.any(live & (nbr_list == position * blocks + 1), axis=1)
    givers = jnp.stack([position ^ 1] + [
        plan[r].giver(position // 2) * 2 + ((position % 2) ^ other) for other in range(2) for r in range(rounds)
    ])
    row_owner = jnp.arange(nbr_list.shape[0]) // blocks
    parity = jnp.any(names_odd[None, :] & (row_owner[None, :] == givers[:, None]), axis=1).astype(jnp.int32)

    gain = gain.reshape(1, width)
    lists = nbr_list.reshape(-1)
    unit, _ = layer_norm(tokens.astype(F32))
    normed = (unit * gain).astype(BF16)
    queries = jnp.dot(normed, w_qkv[:, :width], preferred_element_type=F32).astype(BF16)
    out_grad = dot(cotangent, w_out, 1, 1).astype(BF16)
    arrived[early], parity, lists, gain = lax.optimization_barrier(
        (arrived[early], parity, lists, gain)
    )
    for r in fetch_order:
        passed[r] = lax.ppermute(arrived[r], "seq", mate)
    direct = [r for r in fetch_order if plan[r].source is None]
    relayed = [r for r in fetch_order if plan[r].source is not None]
    windows, places = [tokens], [0]
    for some in (direct, relayed):
        windows += [arrived[r] for r in some]
        places += [2 * (r + 1) for r in some]
        if some is direct:
            windows.append(lax.ppermute(tokens, "seq", mate))
            places.append(1)
        windows += [passed[r] for r in some]
        places += [2 * (r + 1) + 1 for r in some]

    attended, query_grad, own, sib, *messages = main_call(
        chips, position.reshape(1), lists, nbr_count, places, windows, queries, out_grad, gain, w_qkv
    )

    came, sibs = [None] * rounds, [None] * rounds
    first, last = give_order[0], give_order[-1]
    for r in give_order:
        if r == last:
            layer_out, base = middle_call(
                1 + first, parity, came[first], attended, query_grad, own, tokens, w_qkv, w_out
            )
            messages[r], layer_out, base = lax.optimization_barrier((messages[r], layer_out, base))
        came[r] = send(messages[r], plan[r].give)
    came[first], sib = lax.optimization_barrier((came[first], sib))
    sib = lax.ppermute(sib, "seq", mate)
    for r in give_order:
        sibs[r] = lax.ppermute(came[r], "seq", mate)
    token_grad = final_call(give_order, first, parity, came, sibs, sib, base, tokens, cotangent, gain)
    return (layer_out, token_grad)


def solution(mesh):
    in_specs = (
        P(("groups", "seq"), None),
        P(),
        P(),
        P(),
        P("groups", None),
        P("groups"),
        P(("groups", "seq"), None),
    )
    out_specs = (P(("groups", "seq"), None), P(("groups", "seq"), None))
    return jax.shard_map(
        per_device, mesh=mesh, in_specs=in_specs, out_specs=out_specs, check_vma=False
    )
```
